128 devices in a mesh: grp: 32 (over x, z_lo, y), seq: 4 (over z_hi, core).
Axes of the slice: x: 4, y: 4, z: 4 (z_hi: 2, z_lo: 2; z = z_hi * 2 + z_lo), core: 2. Of those that a mesh axis runs over, the one named last changes fastest.
Arguments:
- x_home: bfloat16 [65536, 512], P(('grp', 'seq')), may hold values from -6 to 6
- dy_home: bfloat16 [65536, 512], P(('grp', 'seq')), may hold values from -6 to 6
- w_in: bfloat16 [512, 2048], replicated, may hold values from -0.25 to 0.25
- w_out: bfloat16 [512, 512], replicated, may hold values from -0.25 to 0.25
- place: int32 [32, 4, 512], P('grp', 'seq'), may hold values from 0 to 511, each once within a row
- seg_ids: int32 [32, 2048], P('grp'), may hold values from 0 to 1, as said below
Outputs:
- dx_home: bfloat16 [65536, 512], P(('grp', 'seq'))
- grad_w_in: float32 [512, 2048], replicated
- grad_w_out: float32 [512, 512], replicated
The draws below stay inside these ranges and needn't reach their ends.
Inputs may be any that keep to these rules, and one draw needn't show every extreme that they name: `place`: each device's list names each of its 512 received events once. `seg_ids`: history numbers never fall along a device set; every set has 2 histories, one of exactly 1536 events and one of 512 events, in either order.
All inputs are finite; a program needn't handle non-finite values.
Results may differ from the reference program's by a relative error of at most 0.0075.
Values may be sent and summed in bfloat16 or wider, within the bound.
A program may use at most 192 MiB of HBM per device.

```python
import jax
import jax.numpy as jnp
from jax import lax

HEADS = 8
HEAD_DIM = 64
D = 512
ROWS_DEV = 512
SET_ROWS = 2048
LONGEST = 1536
BLOCK = 16
TOKENS = 65536
N_GRP = 32
N_SEQ = 4


def draw_seg_ids(key, part):
    key = jax.random.fold_in(key, 11)
    flipped = jax.random.randint(key, (N_GRP, 1), 0, 2).astype(jnp.int32)
    first_len = jnp.where(flipped == 1, LONGEST, SET_ROWS - LONGEST).astype(jnp.int32)
    where_all = jnp.arange(SET_ROWS, dtype=jnp.int32)[None, :]
    return (where_all >= first_len).astype(jnp.int32)


def level_of(key, shape, cuts, low, largest):
    gain = 1.0
    for position, shards_of in cuts:
        heights = jax.random.uniform(jax.random.fold_in(jax.random.fold_in(key, 6), position), (shards_of,), jnp.float32, low / len(cuts), largest / len(cuts))
        gain = gain * jnp.repeat(jnp.exp(heights), shape[position] // shards_of).reshape((-1,) + (1,) * (len(shape) - 1 - position))
    return gain


def normal_values(stream_key, extent, scale, most, shards=(), kind=jnp.bfloat16):
    drawn = jax.random.normal(stream_key, extent, jnp.float32) * scale
    if len(shards) > 0:
        drawn = level_of(stream_key, extent, shards, -0.22, 0.18) * drawn
    return jnp.clip(drawn, min=-most, max=most).astype(kind)


def setup_inputs(seed: int = 0) -> dict:
    arg_keys = jax.random.split(jax.random.key(seed), 7)
    x_home = normal_values(arg_keys[0], (TOKENS, D), 1.0, 6.0, ((0, 128),))
    dy_home = normal_values(arg_keys[1], (TOKENS, D), 1.0, 6.0, ((0, 128),))
    w_in = normal_values(arg_keys[2], (D, 4 * D), D ** -0.5, 0.25)
    w_out = normal_values(arg_keys[3], (D, D), D ** -0.5, 0.25)
    place = jax.vmap(lambda own: jax.random.permutation(own, ROWS_DEV))(jax.random.split(arg_keys[4], N_GRP * N_SEQ)).reshape((N_GRP, N_SEQ, ROWS_DEV)).astype(jnp.int32)
    seg_ids = draw_seg_ids(jax.random.fold_in(arg_keys[6], 71), 0)
    return dict(x_home=x_home, dy_home=dy_home, w_in=w_in, w_out=w_out, place=place, seg_ids=seg_ids)


def silu_grad(value):
    sig = jax.nn.sigmoid(value)
    return sig * (1.0 + value * (1.0 - sig))

def reference(x_home, dy_home, w_in, w_out, place, seg_ids):

    def to_owner(home):
        split = home.reshape(N_GRP, N_SEQ, N_GRP, BLOCK, D).transpose(2, 1, 0, 3, 4).reshape(N_GRP, N_SEQ, ROWS_DEV, D)
        index = jnp.broadcast_to(place[..., None], split.shape)
        return jnp.take_along_axis(split, index, axis=2).reshape(N_GRP, SET_ROWS, D)
    x_sets = to_owner(x_home)
    dy_sets = to_owner(dy_home)
    alpha = HEAD_DIM ** (-0.5)

    def one_set(carry, inputs):
        x_rows, dy_rows, segments = inputs
        pre = jnp.dot(x_rows, w_in, preferred_element_type=jnp.float32)
        act = jax.nn.silu(pre).astype(jnp.bfloat16)
        gate_u = act[:, :D].astype(jnp.float32)
        value = act[:, D:2 * D].astype(jnp.float32).reshape(SET_ROWS, HEADS, HEAD_DIM)
        query = act[:, 2 * D:3 * D].astype(jnp.float32).reshape(SET_ROWS, HEADS, HEAD_DIM)
        key = act[:, 3 * D:].astype(jnp.float32).reshape(SET_ROWS, HEADS, HEAD_DIM)
        same = segments[:, None] == segments[None, :]
        where_all = jnp.arange(SET_ROWS, dtype=jnp.int32)
        allowed = same & (where_all[:, None] >= where_all[None, :])
        scale_row = 1.0 / lax.optimization_barrier(jnp.sum(same, axis=1)).astype(jnp.float32)
        scores = jnp.einsum('qhd,khd->hqk', query, key) * alpha
        weight = (jnp.where(allowed[None], jax.nn.silu(scores), 0.0) * scale_row[None, :, None]).astype(jnp.bfloat16)
        weight_f = weight.astype(jnp.float32)
        out = jnp.einsum('hqk,khd->qhd', weight_f, value).reshape(SET_ROWS, D)
        centre = lax.optimization_barrier(jnp.mean(out, axis=-1, keepdims=True))
        centered = out - centre
        spread = lax.rsqrt(lax.optimization_barrier(jnp.mean(centered * centered, axis=-1, keepdims=True)) + 1e-05)
        normed = centered * spread
        mixed = (normed * gate_u).astype(jnp.bfloat16)
        d_mixed = jnp.dot(dy_rows, w_out.T, preferred_element_type=jnp.float32)
        d_gate_u = d_mixed * normed
        d_normed = d_mixed * gate_u
        d_out = (spread * (d_normed - lax.optimization_barrier(jnp.mean(d_normed, axis=-1, keepdims=True)) - normed * lax.optimization_barrier(jnp.mean(d_normed * normed, axis=-1, keepdims=True)))).astype(jnp.bfloat16)
        grad_heads = d_out.astype(jnp.float32).reshape(SET_ROWS, HEADS, HEAD_DIM)
        d_weight = jnp.einsum('qhd,khd->hqk', grad_heads, value)
        d_value = jnp.einsum('hqk,qhd->khd', weight_f, grad_heads).reshape(SET_ROWS, D)
        d_score = (jnp.where(allowed[None], d_weight * silu_grad(scores), 0.0) * scale_row[None, :, None] * alpha).astype(jnp.bfloat16).astype(jnp.float32)
        d_query = jnp.einsum('hqk,khd->qhd', d_score, key).reshape(SET_ROWS, D)
        d_key = jnp.einsum('hqk,qhd->khd', d_score, query).reshape(SET_ROWS, D)
        d_act = jnp.concatenate([d_gate_u, d_value, d_query, d_key], axis=1)
        d_pre = (d_act * silu_grad(pre)).astype(jnp.bfloat16)
        grad_x = (jnp.dot(d_pre, w_in.T, preferred_element_type=jnp.float32) + dy_rows.astype(jnp.float32)).astype(jnp.bfloat16)
        grad_in = carry[0] + jnp.dot(x_rows.T, d_pre, preferred_element_type=jnp.float32)
        grad_out = carry[1] + jnp.dot(mixed.T, dy_rows, preferred_element_type=jnp.float32)
        return ((grad_in, grad_out), grad_x)
    start = (jnp.zeros((D, 4 * D), jnp.float32), jnp.zeros((D, D), jnp.float32))
    (grad_in, grad_out), grads = lax.scan(one_set, start, (x_sets, dy_sets, seg_ids))
    owner = grads.reshape(N_GRP, N_SEQ, ROWS_DEV, D)
    inverse = jnp.argsort(place, axis=2).astype(jnp.int32)
    received = jnp.take_along_axis(owner, jnp.broadcast_to(inverse[..., None], owner.shape), axis=2)
    home = received.reshape(N_GRP, N_SEQ, N_GRP, BLOCK, D).transpose(2, 1, 0, 3, 4).reshape(TOKENS, D)
    factor = TOKENS ** (-0.5)
    return (home, grad_in * factor, grad_out * factor)
```

```python
import jax
import jax.numpy as jnp
from jax import lax
from jax.experimental import pallas as pl
from jax.experimental.pallas import tpu as pltpu
from jax.sharding import PartitionSpec as P

BF = jnp.bfloat16
F32 = jnp.float32
MESH = pl.DeviceIdType.MESH
NN = (((1,), (0,)), ((), ()))
NT = (((1,), (1,)), ((), ()))
TN = (((0,), (0,)), ((), ()))


def mm(a, b, dims=NN):
    return lax.dot_general(a, b, dims, preferred_element_type=F32)


def remote(src, dst, send, recv, device):
    return pltpu.make_async_remote_copy(
        src_ref=src,
        dst_ref=dst,
        send_sem=send,
        recv_sem=recv,
        device_id=device,
        device_id_type=MESH,
    )


def wait_for(ref, sem):
    pltpu.make_async_copy(ref, ref, sem).wait()


def kernel(
    x_ref, dy_ref, win_ref, wout_ref, place_ref, seg_ref,
    dx_out, gin_out, gout_out,
    rows, perm, x_all, dy_all, act, slope, qm, qn, kn, vn, wc, fc, out_u, dm_t, stats,
    dom, don, dv_u, dk_u, dpre, wsl, wt, wo, places,
    ge_s, ge_r, gl_s, gl_r, ag, dxs, dxp, zr, fin,
    local_sem, plane_s, plane_r, z_s, z_r, core_s, core_r, seq_s, seq_r, ge_sem, gl_sem,
    ag_s, ag_r, dxc_s, dxc_r, dxz_s, dxz_r, home_sem,
):
    g = lax.axis_index("grp")
    s = lax.axis_index("seq")
    x, zl, y = g // 8, (g // 4) % 2, g % 4
    zh, c = s // 2, s % 2
    xy = x * 4 + y

    def grp(x_, zl_, y_):
        return (x_ * 2 + zl_) * 4 + y_

    weight_copies = []
    for b in range(4):
        weight_copies.append(
            pltpu.make_async_copy(
                win_ref.at[:, pl.ds(pl.multiple_of(b * 512 + s * 128, 128), 128)],
                wsl.at[:, b * 128 : (b + 1) * 128],
                local_sem.at[b],
            )
        )
    weight_copies.append(
        pltpu.make_async_copy(
            wout_ref.at[pl.ds(pl.multiple_of(s * 128, 128), 128)], wo, local_sem.at[4]
        )
    )
    for copy in weight_copies:
        copy.start()

    barrier = pltpu.get_barrier_semaphore()

    @pl.loop(1, 32)
    def _(i):
        pl.semaphore_signal(
            barrier, inc=1, device_id=(lax.rem(g + i, 32), s), device_id_type=MESH
        )

    for i in range(1, 4):
        pl.semaphore_signal(
            barrier, inc=1, device_id=(g, lax.rem(s + i, 4)), device_id_type=MESH
        )
    pl.semaphore_signal(
        barrier, inc=1, device_id=(grp(x, 1 - zl, y), (1 - zh) * 2 + c), device_id_type=MESH
    )
    pl.semaphore_wait(barrier, 35)

    homes = (x_ref, dy_ref)
    for a in range(2):

        @pl.loop(1, 16)
        def _(i, a=a):
            to = lax.rem(xy + i, 16)
            tx, ty = to // 4, lax.rem(to, 4)
            remote(
                homes[a].at[tx, :, ty],
                rows.at[a, c, pl.ds(zl, 2), zh, xy],
                plane_s.at[a],
                plane_r.at[a],
                (grp(tx, zl, ty), s),
            ).start()

        pltpu.make_async_copy(
            homes[a].at[x, :, y], rows.at[a, c, pl.ds(zl, 2), zh, xy], plane_r.at[a]
        ).start()
        if a == 0:
            pltpu.make_async_copy(place_ref, places.at[s], local_sem.at[5]).start()
            for i in range(1, 4):
                remote(
                    place_ref,
                    places.at[s],
                    seq_s.at[0, i - 1],
                    seq_r.at[0, i - 1],
                    (g, lax.rem(s + i, 4)),
                ).start()

    z_peers = (
        (grp(x, 1 - zl, y), s),
        (grp(x, 1 - zl, y), (1 - zh) * 2 + c),
        (g, (1 - zh) * 2 + c),
    )

    def plane_done(a):
        return rows.at[a, c, pl.ds(zl, 2), zh]

    def block(a, core, zl_, zh_):
        return rows.at[a, core, 2 * zl_, zh_]

    def z_out(a, k):
        src = rows.at[a, c, 1, zh] if k < 2 else block(a, c, zl, zh)
        return remote(
            src, block(a, c, zl, zh), z_s.at[a, k], z_r.at[a, k], z_peers[k]
        )

    where_from = ((1 - zl, zh), (1 - zl, 1 - zh), (zl, 1 - zh), (zl, zh))

    def core_out(a, k):
        ref = block(a, c, *where_from[k])
        return remote(ref, ref, core_s.at[a, k], core_r.at[a, k], (g, zh * 2 + 1 - c))

    def spread_plane(a):
        wait_for(plane_done(a), plane_r.at[a])
        for k in range(3):
            z_out(a, k).start()
        core_out(a, 3).start()

    def forward(a):
        for k in range(3):
            wait_for(block(a, c, *where_from[k]), z_r.at[a, k])
            core_out(a, k).start()

    def from_core(a):
        for k in range(4):
            wait_for(block(a, 1 - c, *where_from[k]), core_r.at[a, k])

    for copy in weight_copies:
        copy.wait()
    wt[...] = wsl[...].T
    spread_plane(0)

    wait_for(places.at[0], local_sem.at[5])
    for i in range(1, 4):
        wait_for(places.at[0], seq_r.at[0, i - 1])

    def slot_of(p):
        return ((p >> 6) & 1) * 256 + (p >> 7) * 64 + (p & 63)

    @pl.loop(0, 4)
    def _(q):
        slot = slot_of(places[q])
        column = jnp.broadcast_to(slot.astype(F32), (128, 512)).T
        lane = lax.broadcasted_iota(jnp.int32, (512, 128), 1).astype(F32)
        for b in range(4):
            perm[q, :, b * 128 : (b + 1) * 128] = jnp.where(
                column == lane + float(b * 128), 1.0, 0.0
            ).astype(BF)

    def ordered(a, q):
        low = rows[a, lax.rem(q, 2), 0, q // 2].reshape(256, 512)
        high = rows[a, lax.rem(q, 2), 2, q // 2].reshape(256, 512)
        return (mm(perm[q, :, :256], low) + mm(perm[q, :, 256:], high)).astype(BF)

    spread_plane(1)
    forward(0)
    from_core(0)

    @pl.loop(0, 4)
    def _(q):
        x_all[q] = ordered(0, q)
        for b in range(4):
            pre = mm(wt[b * 128 : (b + 1) * 128, :], x_all[q], NT)
            sig = 0.5 * jnp.tanh(0.5 * pre) + 0.5
            full = pre * sig
            slope[q, b * 128 : (b + 1) * 128, :] = sig + full * (1.0 - sig)
            cut = full.astype(BF)
            act[q, b * 128 : (b + 1) * 128, :] = cut
            if b == 1:
                vn[q] = cut.T
            if b == 2:
                qn[q] = (cut * BF(0.125)).T
                scaled = cut * BF(0.0625)
                zero = jnp.zeros((64, 512), BF)
                qm[q, 0] = jnp.concatenate([scaled[:64], zero], axis=0)
                qm[q, 1] = jnp.concatenate([zero, scaled[64:]], axis=0)
            if b == 3:
                kn[q] = cut.T

    forward(1)

    is_a = seg_ref[0, 0] == seg_ref[0, 1535]
    in_a = jnp.where(is_a, 1.0, 0.0).astype(F32)
    in_b = 1.0 - in_a
    long, short = 1.0 / 1536.0, 1.0 / 512.0
    inv_len = (
        in_a * long + in_b * short, long, long, in_a * short + in_b * long
    )

    def query_of(f):
        return jnp.where(f == 2, 2, jnp.where(is_a, f + 1, 3))

    def key_of(f):
        return jnp.where(f == 2, 1, jnp.where(is_a, 0, 2 - f))

    def causal(rows_, cols):
        return lax.broadcasted_iota(jnp.int32, (rows_, cols), 0) <= lax.broadcasted_iota(
            jnp.int32, (rows_, cols), 1
        )

    def weigh(u, qi, ki, head, half, first, masked):
        keys = pl.ds(half * 256, 256)
        h = mm(kn[ki, keys, :], qm[qi, head, :, first:])
        t = jnp.tanh(h)
        a = 1.0 + t
        w = h * a
        f = a * (1.0 - w) + (w + w)
        if masked:
            keep = causal(256, 512 - first)
            w = jnp.where(keep, w, 0.0)
            f = jnp.where(keep, f, 0.0)
        w = w.astype(BF)
        wc[u, head, keys, first:] = w
        fc[u, head, keys, first:] = f.astype(BF)
        return mm(act[ki, 128 + head * 64 : 192 + head * 64, keys], w)

    @pl.loop(0, 4)
    def _(q):
        for head in range(2):
            lanes = slice(head * 64, head * 64 + 64)
            out_u[q, lanes, :] = weigh(q, q, q, head, 0, 0, True)
            out_u[q, lanes, 256:] += weigh(q, q, q, head, 1, 256, True)

    @pl.loop(0, 3)
    def _(f):
        qi, ki = query_of(f), key_of(f)
        for head in range(2):
            lanes = slice(head * 64, head * 64 + 64)
            out_u[4 + f, lanes, :] = weigh(4 + f, qi, ki, head, 0, 0, False) + weigh(
                4 + f, qi, ki, head, 1, 0, False
            )

    from_core(1)

    @pl.loop(0, 4)
    def _(q):
        dy_all[q] = ordered(1, q)
        dm_t[q] = mm(wo[...], dy_all[q], NT)

    for q in range(4):
        total = out_u[q]
        if q == 1:
            total = total + in_a * out_u[4]
        if q == 2:
            total = total + out_u[6] + in_a * out_u[5]
        if q == 3:
            total = total + in_b * (out_u[4] + out_u[5])
        total = total * inv_len[q]
        out_u[q] = total
        centre = jnp.mean(total, axis=0, keepdims=True)
        away = total - centre
        d_normed = dm_t[q] * act[q, :128, :].astype(F32)
        stats[s, 0, q : q + 1, :] = centre
        stats[s, 1, q : q + 1, :] = jnp.sum(away * away, axis=0, keepdims=True)
        stats[s, 2, q : q + 1, :] = jnp.sum(d_normed, axis=0, keepdims=True)
        stats[s, 3, q : q + 1, :] = jnp.sum(d_normed * away, axis=0, keepdims=True)

    def stats_out(i):
        return remote(
            stats.at[s], stats.at[s], seq_s.at[1, i - 1], seq_r.at[1, i - 1],
            (g, lax.rem(s + i, 4)),
        )

    for i in range(1, 4):
        stats_out(i).start()
    for i in range(1, 4):
        wait_for(stats.at[lax.rem(s + i, 4)], seq_r.at[1, 3 - i])

    centres = [stats[r, 0] for r in range(4)]
    mean_all = (centres[0] + centres[1] + centres[2] + centres[3]) * 0.25
    square = jnp.zeros_like(mean_all)
    plain = jnp.zeros_like(mean_all)
    cross = jnp.zeros_like(mean_all)
    for r in range(4):
        off = centres[r] - mean_all
        square += stats[r, 1] + 128.0 * off * off
        plain += stats[r, 2]
        cross += stats[r, 3] + off * stats[r, 2]
    spread_all = lax.rsqrt(square * (1.0 / 512.0) + 1e-5)
    plain = plain * (1.0 / 512.0)
    cross = cross * spread_all * (1.0 / 512.0)

    grad_out = jnp.zeros((128, 512), F32)
    grad_u = jnp.zeros((128, 512), F32)
    for q in range(4):
        gate = act[q, :128, :].astype(F32)
        spread = spread_all[q : q + 1]
        normed = (out_u[q] - mean_all[q : q + 1]) * spread
        d_mixed = dm_t[q]
        mixed = (normed * gate).astype(BF)
        d_u = (d_mixed * normed * slope[q, :128, :]).astype(BF)
        dpre[q, :128, :] = d_u
        d_out = (
            (d_mixed * gate - plain[q : q + 1] - normed * cross[q : q + 1])
            * (spread * (0.5 * inv_len[q]))
        ).astype(BF)
        zero = jnp.zeros((64, 512), BF)
        dom[q, 0] = jnp.concatenate([d_out[:64], zero], axis=0)
        dom[q, 1] = jnp.concatenate([zero, d_out[64:]], axis=0)
        don[q] = d_out.T
        grad_out += mm(mixed, dy_all[q])
        grad_u += mm(d_u, x_all[q])

    def grads_out(buf, got, sem):
        @pl.loop(1, 32)
        def _(i):
            to = lax.rem(g + i, 32)
            remote(buf.at[to], got.at[g], sem.at[0], sem.at[1], (to, s)).start()

        pltpu.make_async_copy(buf.at[g], got.at[g], sem.at[1]).start()

    ge_s[:, 0] = grad_u.T.astype(BF).reshape(32, 16, 128)
    for b in range(4):
        ge_s[8 * b : 8 * b + 8, 1] = (
            grad_out[:, b * 128 : (b + 1) * 128].astype(BF).reshape(8, 16, 128)
        )
    grads_out(ge_s, ge_r, ge_sem)

    def attend_back(u, qi, ki, masked):
        lane = lax.broadcasted_iota(jnp.int32, (256, 128), 1)
        d_q = [None, None]
        for half in range(2):
            keys = pl.ds(half * 256, 256)
            first = 256 if masked and half == 1 else 0
            d_v, d_k = [], []
            for head in range(2):
                d_w = mm(vn[ki, keys, :], dom[qi, head, :, first:])
                d_s = (d_w * fc[u, head, keys, first:].astype(F32)).astype(BF)
                d_v.append(mm(wc[u, head, keys, first:], don[qi, first:, :]))
                d_k.append(mm(d_s, qn[qi, first:, :]))
                part = mm(act[ki, 384 + head * 64 : 448 + head * 64, keys], d_s)
                lanes = slice(head * 64, head * 64 + 64)
                if half == 0:
                    out_u[u, lanes, :] = part
                else:
                    out_u[u, lanes, first:] += part
            dv_u[u, keys, :] = jnp.where(lane < 64, d_v[0], d_v[1])
            dk_u[u, keys, :] = jnp.where(lane < 64, d_k[0], d_k[1])

    @pl.loop(0, 4)
    def _(q):
        attend_back(q, q, q, True)

    @pl.loop(0, 3)
    def _(f):
        attend_back(4 + f, query_of(f), key_of(f), False)

    for q in range(4):
        d_q, d_k, d_v = out_u[q], dk_u[q], dv_u[q]
        if q == 0:
            d_k = d_k + in_a * (dk_u[4] + dk_u[5])
            d_v = d_v + in_a * (dv_u[4] + dv_u[5])
        if q == 1:
            d_q = d_q + in_a * out_u[4]
            d_k = d_k + dk_u[6] + in_b * dk_u[5]
            d_v = d_v + dv_u[6] + in_b * dv_u[5]
        if q == 2:
            d_q = d_q + out_u[6] + in_a * out_u[5]
            d_k = d_k + in_b * dk_u[4]
            d_v = d_v + in_b * dv_u[4]
        if q == 3:
            d_q = d_q + in_b * (out_u[4] + out_u[5])
        dpre[q, 128:256, :] = (2.0 * d_v.T * slope[q, 128:256, :]).astype(BF)
        dpre[q, 256:384, :] = (0.125 * d_q * slope[q, 256:384, :]).astype(BF)
        dpre[q, 384:512, :] = (d_k.T * slope[q, 384:512, :]).astype(BF)

    def partial(q):
        return mm(dpre[q], wt[...], TN)

    def dx_core(k):
        return remote(
            dxs.at[k], dxp.at[k], dxc_s.at[k], dxc_r.at[k], (g, zh * 2 + 1 - c)
        )

    for k in range(2):
        dxs[k] = partial(2 * k + 1 - c).astype(BF)
        dx_core(k).start()

    for b in range(1, 4):
        total = jnp.zeros((128, 512), F32)
        for q in range(4):
            total += mm(dpre[q, b * 128 : (b + 1) * 128, :], x_all[q])
        gl_s[:, b - 1] = total.T.astype(BF).reshape(32, 16, 128)

    def dx_z(k, src):
        return remote(src, zr.at[k], dxz_s.at[k], dxz_r.at[k], z_peers[k])

    for k in range(2):
        k_zh = lax.rem(zh + 1 + k, 2)
        q = k_zh * 2 + c
        mine = partial(q)
        mine = mine + jnp.where(q == s, 1.0, 0.0) * dy_all[q].astype(F32)
        wait_for(dxp.at[k_zh], dxc_r.at[k_zh])
        both = (mine + dxp[k_zh].astype(F32)).astype(BF)
        slot = slot_of(places[q])
        back = jnp.where(
            lax.broadcasted_iota(jnp.int32, (512, 512), 0) == slot, 1.0, 0.0
        ).astype(BF)
        dxs[2 + k] = mm(back, both).astype(BF)
        half_mine = pl.ds(pl.multiple_of(zl * 256, 256), 256)
        half_other = pl.ds(pl.multiple_of((1 - zl) * 256, 256), 256)
        if k == 0:
            dx_z(2, dxs.at[2, half_mine]).start()
            dx_z(1, dxs.at[2, half_other]).start()
        else:
            dx_z(0, dxs.at[3, half_other]).start()

    grads_out(gl_s, gl_r, gl_sem)

    for k in range(3):
        wait_for(zr.at[k], dxz_r.at[k])
    own = (
        dxs[3, pl.ds(pl.multiple_of(zl * 256, 256), 256)].astype(F32) + zr[2].astype(F32)
    ).astype(BF)
    other = (zr[0].astype(F32) + zr[1].astype(F32)).astype(BF)
    fin[pl.ds(zl, 1)] = own.reshape(1, 16, 16, 512)
    fin[pl.ds(1 - zl, 1)] = other.reshape(1, 16, 16, 512)

    @pl.loop(1, 16)
    def _(i):
        to = lax.rem(xy + i, 16)
        tx, ty = to // 4, lax.rem(to, 4)
        remote(
            fin.at[:, to], dx_out.at[x, :, y], home_sem.at[0], home_sem.at[1],
            (grp(tx, zl, ty), s),
        ).start()

    pltpu.make_async_copy(fin.at[:, xy], dx_out.at[x, :, y], home_sem.at[1]).start()

    first = jnp.where(c == 0, x, y)
    second = jnp.where(c == 0, y, x)
    zz = zl * 2 + zh
    wait_for(ge_r, ge_sem.at[1])
    wait_for(gl_r, gl_sem.at[1])
    early = jnp.sum(ge_r[...].astype(F32), axis=0)
    late = jnp.sum(gl_r[...].astype(F32), axis=0)
    here = ag.at[c, first, second, zz]
    here[0:1] = early[0:1].astype(BF)
    here[1:4] = late.astype(BF)
    here[4:5] = early[1:2].astype(BF)

    def spread_ag(phase, ref, peers):
        copies = [
            remote(ref, ref, ag_s.at[phase, k], ag_r.at[phase, k], peer)
            for k, peer in enumerate(peers)
        ]
        for copy in copies:
            copy.start()
        for k in range(len(peers)):
            wait_for(ref, ag_r.at[phase, k])
        return copies

    def along(i, on_first):
        nf = lax.rem(first + i, 4) if on_first else first
        ns = second if on_first else lax.rem(second + i, 4)
        nx = jnp.where(c == 0, nf, ns)
        ny = jnp.where(c == 0, ns, nf)
        return (grp(nx, zl, ny), s)

    ag_copies = spread_ag(0, here, z_peers)
    ag_copies += spread_ag(
        1, ag.at[c, first, second], [along(i, False) for i in range(1, 4)]
    )
    ag_copies += spread_ag(2, ag.at[c, first], [along(i, True) for i in range(1, 4)])
    ag_copies += spread_ag(3, ag.at[c], [(g, zh * 2 + 1 - c)])

    factor = 1.0 / 256.0
    for cc in range(2):
        for z in range(4):
            zl_, zh_ = z // 2, z % 2
            s_ = zh_ * 2 + cc
            for x_ in range(4):

                @pl.loop(0, 4)
                def _(y_, cc=cc, z=z, x_=x_, zl_=zl_, s_=s_):
                    f_, n_ = (x_, y_) if cc == 0 else (y_, x_)
                    group = grp(x_, zl_, y_)
                    at = pl.ds(pl.multiple_of(group * 16, 16), 16)
                    for b in range(4):
                        lo = b * 512 + s_ * 128
                        gin_out[at, lo : lo + 128] = ag[cc, f_, n_, z, b].astype(F32) * factor
                    at = pl.ds(pl.multiple_of(s_ * 128 + (zl_ * 4 + y_) * 16, 16), 16)
                    gout_out[at, x_ * 128 : x_ * 128 + 128] = (
                        ag[cc, f_, n_, z, 4].astype(F32) * factor
                    )

    wait_for(dx_out, home_sem.at[1])
    wait_for(fin.at[:, 0:15], home_sem.at[0])
    for copy in ag_copies:
        copy.wait_send()
    for a in range(2):
        wait_for(rows.at[a, c, 0:2, 0, 0:15], plane_s.at[a])
        for k in range(3):
            z_out(a, k).wait_send()
        for k in range(4):
            core_out(a, k).wait_send()
    for i in range(1, 4):
        wait_for(places.at[0], seq_s.at[0, i - 1])
        stats_out(i).wait_send()
    for k in range(2):
        dx_core(k).wait_send()
    for k in range(3):
        wait_for(zr.at[k], dxz_s.at[k])
    wait_for(ge_s.at[0:31], ge_sem.at[0])
    wait_for(gl_s.at[0:31], gl_sem.at[0])


def per_device(x_home, dy_home, w_in, w_out, place, seg_ids):
    shape = (4, 2, 4, 16, 512)
    vm = pltpu.VMEM
    dma = pltpu.SemaphoreType.DMA
    hbm = pl.BlockSpec(memory_space=pl.ANY)
    in_vmem = pl.BlockSpec(memory_space=pltpu.VMEM)
    dx, g_in, g_out = pl.pallas_call(
        kernel,
        out_shape=(
            jax.ShapeDtypeStruct(shape, BF),
            jax.ShapeDtypeStruct((512, 2048), F32),
            jax.ShapeDtypeStruct((512, 512), F32),
        ),
        in_specs=[
            hbm, hbm, hbm, hbm, in_vmem, pl.BlockSpec(memory_space=pltpu.SMEM),
        ],
        out_specs=(hbm, in_vmem, in_vmem),
        scratch_shapes=[
            vm((2, 2, 3, 2, 16, 16, 512), BF),
            vm((4, 512, 512), BF),
            vm((4, 512, 512), BF),
            vm((4, 512, 512), BF),
            vm((4, 512, 512), BF),
            vm((4, 512, 512), F32),
            vm((4, 2, 128, 512), BF),
            vm((4, 512, 128), BF),
            vm((4, 512, 128), BF),
            vm((4, 512, 128), BF),
            vm((7, 2, 512, 512), BF),
            vm((7, 2, 512, 512), BF),
            vm((7, 128, 512), F32),
            vm((4, 128, 512), F32),
            vm((4, 4, 4, 512), F32),
            vm((4, 2, 128, 512), BF),
            vm((4, 512, 128), BF),
            vm((7, 512, 128), F32),
            vm((7, 512, 128), F32),
            vm((4, 512, 512), BF),
            vm((512, 512), BF),
            vm((512, 512), BF),
            vm((128, 512), BF),
            vm((4, 1, 512), jnp.int32),
            vm((32, 2, 16, 128), BF),
            vm((32, 2, 16, 128), BF),
            vm((32, 3, 16, 128), BF),
            vm((32, 3, 16, 128), BF),
            vm((2, 4, 4, 4, 5, 16, 128), BF),
            vm((4, 512, 512), BF),
            vm((2, 512, 512), BF),
            vm((3, 256, 512), BF),
            vm((2, 16, 16, 512), BF),
            dma((6,)), dma((2,)), dma((2,)), dma((2, 3)), dma((2, 3)), dma((2, 4)),
            dma((2, 4)), dma((2, 3)), dma((2, 3)), dma((2,)), dma((2,)),
            dma((4, 3)), dma((4, 3)), dma((2,)), dma((2,)), dma((3,)), dma((3,)), dma((2,)),
        ],
        compiler_params=pltpu.CompilerParams(
            collective_id=0, has_side_effects=True, vmem_limit_bytes=63 * 2**20
        ),
    )(
        x_home.reshape(shape),
        dy_home.reshape(shape),
        w_in,
        w_out,
        place.reshape(1, 512),
        seg_ids.reshape(1, 2048),
    )
    return dx.reshape(512, 512), g_in, g_out


def solution(mesh):
    in_specs = (
        P(("grp", "seq"), None),
        P(("grp", "seq"), None),
        P(),
        P(),
        P("grp", "seq", None),
        P("grp", None),
    )
    out_specs = (P(("grp", "seq"), None), P(), P())
    return jax.shard_map(
        per_device, mesh=mesh, in_specs=in_specs, out_specs=out_specs, check_vma=False
    )
```

```python
import jax
import jax.numpy as jnp
from jax import lax
from jax.experimental import pallas as pl
from jax.experimental.pallas import tpu as pltpu
from jax.sharding import PartitionSpec as P

BF = jnp.bfloat16
F32 = jnp.float32
MESH = pl.DeviceIdType.MESH
NN = (((1,), (0,)), ((), ()))
NT = (((1,), (1,)), ((), ()))
TN = (((0,), (0,)), ((), ()))


def mm(a, b, dims=NN):
    return lax.dot_general(a, b, dims, preferred_element_type=F32)


def remote(src, dst, send, recv, device):
    return pltpu.make_async_remote_copy(
        src_ref=src,
        dst_ref=dst,
        send_sem=send,
        recv_sem=recv,
        device_id=device,
        device_id_type=MESH,
    )


def wait_for(ref, sem):
    pltpu.make_async_copy(ref, ref, sem).wait()


def kernel(
    x_ref, dy_ref, win_ref, wout_ref, place_ref, seg_ref,
    dx_out, age, agl,
    rows, perm, x_all, dy_all, act, slope, qm, qn, kn, vn, wc, fc, out_u, dm_t, stats,
    dom, don, dv_u, dk_u, dpre, wsl, wt, wo, places,
    ge_s, ge_r, gl_s, gl_r, met_e, mine_e, met_l, mine_l, acc, dxs, dxp, zr, fin,
    local_sem, plane_s, plane_r, z_s, z_r, core_s, core_r, seq_s, seq_r, ge_sem, gl_sem,
    ag_s, ag_r, ag_l, dxc_s, dxc_r, dxz_s, dxz_r, home_sem,
):
    g = lax.axis_index("grp")
    s = lax.axis_index("seq")
    x, zl, y = g // 8, (g // 4) % 2, g % 4
    zh, c = s // 2, s % 2

    def grp(x_, zl_, y_):
        return (x_ * 2 + zl_) * 4 + y_

    weight_copies = []
    for b in range(4):
        weight_copies.append(
            pltpu.make_async_copy(
                win_ref.at[:, pl.ds(pl.multiple_of(b * 512 + s * 128, 128), 128)],
                wsl.at[:, b * 128 : (b + 1) * 128],
                local_sem.at[b],
            )
        )
    weight_copies.append(
        pltpu.make_async_copy(
            wout_ref.at[pl.ds(pl.multiple_of(s * 128, 128), 128)], wo, local_sem.at[4]
        )
    )
    for copy in weight_copies:
        copy.start()

    barrier = pltpu.get_barrier_semaphore()

    def shifted(i, sign):
        return lax.rem(x + 4 + sign * (i // 4), 4), lax.rem(y + 4 + sign * lax.rem(i, 4), 4)

    @pl.loop(1, 16)
    def _(i):
        tx, ty = shifted(i, 1)
        pl.semaphore_signal(
            barrier, inc=1, device_id=(grp(tx, zl, ty), s), device_id_type=MESH
        )

    for i in range(1, 4):
        pl.semaphore_signal(
            barrier, inc=1, device_id=(g, lax.rem(s + i, 4)), device_id_type=MESH
        )
    for to_zh in range(2):
        pl.semaphore_signal(
            barrier, inc=1, device_id=(grp(x, 1 - zl, y), to_zh * 2 + c), device_id_type=MESH
        )
    pl.semaphore_wait(barrier, 20)

    homes = (x_ref, dy_ref)
    for a in range(2):
        for h in range(2):

            @pl.loop(1 - h, 8)
            def _(j, a=a, h=h):
                i = j + 8 * h
                tx, ty = shifted(i, 1)
                remote(
                    homes[a].at[tx, :, ty],
                    rows.at[a, c, pl.ds(zl, 2), zh, i],
                    plane_s.at[a],
                    plane_r.at[a, h],
                    (grp(tx, zl, ty), s),
                ).start()

            if h == 0:
                pltpu.make_async_copy(
                    homes[a].at[x, :, y], rows.at[a, c, pl.ds(zl, 2), zh, 0], plane_r.at[a, 0]
                ).start()
        if a == 0:
            pltpu.make_async_copy(place_ref, places.at[s], local_sem.at[5]).start()
            for i in range(1, 4):
                remote(
                    place_ref,
                    places.at[s],
                    seq_s.at[0, i - 1],
                    seq_r.at[0, i - 1],
                    (g, lax.rem(s + i, 4)),
                ).start()

    z_peers = (
        (grp(x, 1 - zl, y), s),
        (grp(x, 1 - zl, y), (1 - zh) * 2 + c),
        (g, (1 - zh) * 2 + c),
    )

    def slots(h):
        return slice(8 * h, 8 * h + 8)

    def block(a, core, zl_, zh_, h):
        return rows.at[a, core, 2 * zl_, zh_, slots(h)]

    def z_out(a, k, h):
        src = rows.at[a, c, 1, zh, slots(h)] if k < 2 else block(a, c, zl, zh, h)
        return remote(
            src, block(a, c, zl, zh, h), z_s.at[a, k, h], z_r.at[a, k, h], z_peers[k]
        )

    where_from = ((1 - zl, zh), (1 - zl, 1 - zh), (zl, 1 - zh), (zl, zh))

    def core_out(a, k, h):
        ref = block(a, c, *where_from[k], h)
        return remote(
            ref, ref, core_s.at[a, k, h], core_r.at[a, k, h], (g, zh * 2 + 1 - c)
        )

    def spread_plane(a, h):
        wait_for(rows.at[a, c, pl.ds(zl, 2), zh, slots(h)], plane_r.at[a, h])
        for k in range(3):
            z_out(a, k, h).start()
        core_out(a, 3, h).start()

    def forward(a, k, h):
        wait_for(block(a, c, *where_from[k], h), z_r.at[a, k, h])
        core_out(a, k, h).start()

    def from_core(a, k):
        for h in range(2):
            wait_for(block(a, 1 - c, *where_from[k], h), core_r.at[a, k, h])

    for copy in weight_copies:
        copy.wait()
    wt[...] = wsl[...].T
    spread_plane(0, 0)
    spread_plane(0, 1)

    wait_for(places.at[0], local_sem.at[5])
    for i in range(1, 4):
        wait_for(places.at[0], seq_r.at[0, i - 1])

    def slot_of(p):
        apart = ((x - (p >> 7)) & 3) * 4 + ((y - (p >> 4)) & 3)
        return ((p >> 6) & 1) * 256 + apart * 16 + (p & 15)

    @pl.loop(0, 4)
    def _(q):
        slot = slot_of(places[q])
        column = jnp.broadcast_to(slot.astype(F32), (128, 512)).T
        lane = lax.broadcasted_iota(jnp.int32, (512, 128), 1).astype(F32)
        for b in range(4):
            perm[q, :, b * 128 : (b + 1) * 128] = jnp.where(
                column == lane + float(b * 128), 1.0, 0.0
            ).astype(BF)

    def ordered(a, q):
        low = rows[a, lax.rem(q, 2), 0, q // 2].reshape(256, 512)
        high = rows[a, lax.rem(q, 2), 2, q // 2].reshape(256, 512)
        return (mm(perm[q, :, :256], low) + mm(perm[q, :, 256:], high)).astype(BF)

    def project(q):
        x_all[q] = ordered(0, q)
        for b in range(4):
            pre = mm(wt[b * 128 : (b + 1) * 128, :], x_all[q], NT)
            sig = 0.5 * jnp.tanh(0.5 * pre) + 0.5
            full = pre * sig
            slope[q, b * 128 : (b + 1) * 128, :] = sig + full * (1.0 - sig)
            cut = full.astype(BF)
            act[q, b * 128 : (b + 1) * 128, :] = cut
            if b == 1:
                vn[q] = cut.T
            if b == 2:
                qn[q] = (cut * BF(0.125)).T
                scaled = cut * BF(0.0625)
                zero = jnp.zeros((64, 512), BF)
                qm[q, 0] = jnp.concatenate([scaled[:64], zero], axis=0)
                qm[q, 1] = jnp.concatenate([zero, scaled[64:]], axis=0)
            if b == 3:
                kn[q] = cut.T

    is_a = seg_ref[0, 0] == seg_ref[0, 1535]
    in_a = jnp.where(is_a, 1.0, 0.0).astype(F32)
    in_b = 1.0 - in_a
    long, short = 1.0 / 1536.0, 1.0 / 512.0
    inv_len = (
        in_a * long + in_b * short, long, long, in_a * short + in_b * long
    )

    def query_of(f):
        return jnp.where(f == 2, 2, jnp.where(is_a, f + 1, 3))

    def key_of(f):
        return jnp.where(f == 2, 1, jnp.where(is_a, 0, 2 - f))

    def causal(rows_, cols):
        return lax.broadcasted_iota(jnp.int32, (rows_, cols), 0) <= lax.broadcasted_iota(
            jnp.int32, (rows_, cols), 1
        )

    def weigh(u, qi, ki, head, half, first, masked):
        keys = pl.ds(half * 256, 256)
        h = mm(kn[ki, keys, :], qm[qi, head, :, first:])
        t = jnp.tanh(h)
        a = 1.0 + t
        w = h * a
        f = a * (1.0 - w) + (w + w)
        if masked:
            keep = causal(256, 512 - first)
            w = jnp.where(keep, w, 0.0)
            f = jnp.where(keep, f, 0.0)
        w = w.astype(BF)
        wc[u, head, keys, first:] = w
        fc[u, head, keys, first:] = f.astype(BF)
        return mm(act[ki, 128 + head * 64 : 192 + head * 64, keys], w)

    def diagonal(q):
        for head in range(2):
            lanes = slice(head * 64, head * 64 + 64)
            out_u[q, lanes, :] = weigh(q, q, q, head, 0, 0, True)
            out_u[q, lanes, 256:] += weigh(q, q, q, head, 1, 256, True)

    forward(0, 0, 0)
    forward(0, 0, 1)
    spread_plane(1, 0)
    forward(0, 1, 0)
    forward(0, 2, 0)
    spread_plane(1, 1)
    from_core(0, 3)
    from_core(0, 0)

    @pl.loop(0, 2)
    def _(j):
        project(zh * 2 + j)

    forward(0, 1, 1)
    forward(0, 2, 1)

    @pl.loop(0, 2)
    def _(j):
        diagonal(zh * 2 + j)

    from_core(0, 1)
    from_core(0, 2)

    @pl.loop(0, 2)
    def _(j):
        project((1 - zh) * 2 + j)

    forward(1, 0, 0)
    forward(1, 0, 1)

    @pl.loop(0, 2)
    def _(j):
        diagonal((1 - zh) * 2 + j)

    @pl.loop(0, 3)
    def _(f):
        qi, ki = query_of(f), key_of(f)
        for head in range(2):
            lanes = slice(head * 64, head * 64 + 64)
            out_u[4 + f, lanes, :] = weigh(4 + f, qi, ki, head, 0, 0, False) + weigh(
                4 + f, qi, ki, head, 1, 0, False
            )

    def mix_back(q):
        dy_all[q] = ordered(1, q)
        dm_t[q] = mm(wo[...], dy_all[q], NT)

    from_core(1, 3)
    from_core(1, 0)

    @pl.loop(0, 2)
    def _(j):
        mix_back(zh * 2 + j)

    for h in range(2):
        forward(1, 1, h)
        forward(1, 2, h)
    from_core(1, 1)
    from_core(1, 2)

    @pl.loop(0, 2)
    def _(j):
        mix_back((1 - zh) * 2 + j)

    for q in range(4):
        total = out_u[q]
        if q == 1:
            total = total + in_a * out_u[4]
        if q == 2:
            total = total + out_u[6] + in_a * out_u[5]
        if q == 3:
            total = total + in_b * (out_u[4] + out_u[5])
        total = total * inv_len[q]
        out_u[q] = total
        centre = jnp.mean(total, axis=0, keepdims=True)
        away = total - centre
        d_normed = dm_t[q] * act[q, :128, :].astype(F32)
        stats[s, 0, q : q + 1, :] = centre
        stats[s, 1, q : q + 1, :] = jnp.sum(away * away, axis=0, keepdims=True)
        stats[s, 2, q : q + 1, :] = jnp.sum(d_normed, axis=0, keepdims=True)
        stats[s, 3, q : q + 1, :] = jnp.sum(d_normed * away, axis=0, keepdims=True)

    def stats_out(i):
        return remote(
            stats.at[s], stats.at[s], seq_s.at[1, i - 1], seq_r.at[1, i - 1],
            (g, lax.rem(s + i, 4)),
        )

    for i in range(1, 4):
        stats_out(i).start()
    for i in range(1, 4):
        wait_for(stats.at[lax.rem(s + i, 4)], seq_r.at[1, 3 - i])

    centres = [stats[r, 0] for r in range(4)]
    mean_all = (centres[0] + centres[1] + centres[2] + centres[3]) * 0.25
    square = jnp.zeros_like(mean_all)
    plain = jnp.zeros_like(mean_all)
    cross = jnp.zeros_like(mean_all)
    for r in range(4):
        off = centres[r] - mean_all
        square += stats[r, 1] + 128.0 * off * off
        plain += stats[r, 2]
        cross += stats[r, 3] + off * stats[r, 2]
    spread_all = lax.rsqrt(square * (1.0 / 512.0) + 1e-5)
    plain = plain * (1.0 / 512.0)
    cross = cross * spread_all * (1.0 / 512.0)

    grad_out = jnp.zeros((128, 512), F32)
    grad_u = jnp.zeros((128, 512), F32)
    for q in range(4):
        gate = act[q, :128, :].astype(F32)
        spread = spread_all[q : q + 1]
        normed = (out_u[q] - mean_all[q : q + 1]) * spread
        d_mixed = dm_t[q]
        mixed = (normed * gate).astype(BF)
        d_u = (d_mixed * normed * slope[q, :128, :]).astype(BF)
        dpre[q, :128, :] = d_u
        d_out = (
            (d_mixed * gate - plain[q : q + 1] - normed * cross[q : q + 1])
            * (spread * (0.5 * inv_len[q]))
        ).astype(BF)
        zero = jnp.zeros((64, 512), BF)
        dom[q, 0] = jnp.concatenate([d_out[:64], zero], axis=0)
        dom[q, 1] = jnp.concatenate([zero, d_out[64:]], axis=0)
        don[q] = d_out.T
        grad_out += mm(mixed, dy_all[q])
        grad_u += mm(d_u, x_all[q])

    def grads_out(buf, got, sem):
        @pl.loop(1, 16)
        def _(i):
            tx, ty = shifted(i, 1)
            remote(
                buf.at[tx, :, ty], got.at[i], sem.at[0], sem.at[1], (grp(tx, zl, ty), s)
            ).start()

        pltpu.make_async_copy(buf.at[x, :, y], got.at[0], sem.at[1]).start()

    ge_s[:, :, :, 0] = grad_u.T.astype(BF).reshape(4, 2, 4, 16, 128)
    for b in range(4):
        ge_s[b, :, :, 1] = (
            grad_out[:, b * 128 : (b + 1) * 128].astype(BF).reshape(2, 4, 16, 128)
        )
    grads_out(ge_s, ge_r, ge_sem)

    first = jnp.where(c == 0, x, y)
    second = jnp.where(c == 0, y, x)
    zz = zl * 2 + zh
    reduced = ((ge_r, ge_sem), (gl_r, gl_sem))
    met = (met_e, met_l)
    summed = (mine_e, mine_l)
    gathered = (age, agl)

    def z_copies(t):
        ref = met[t].at[zz]
        return [
            remote(ref, ref, ag_s.at[t, 0, k], ag_r.at[t, 0, k], peer)
            for k, peer in enumerate(z_peers)
        ]

    def meet(t):
        got, sem = reduced[t]
        wait_for(got, sem.at[1])
        met[t][zz] = jnp.sum(got[...].astype(F32), axis=0)
        for copy in z_copies(t):
            copy.start()

    def along(i, on_first):
        nf = lax.rem(first + i, 4) if on_first else first
        ns = second if on_first else lax.rem(second + i, 4)
        nx = jnp.where(c == 0, nf, ns)
        ny = jnp.where(c == 0, ns, nf)
        return (grp(nx, zl, ny), s)

    def own_copy(t):
        return pltpu.make_async_copy(
            summed[t], gathered[t].at[c, first, second], ag_l.at[t]
        )

    def second_copies(t):
        return [
            remote(
                summed[t], gathered[t].at[c, first, second],
                ag_s.at[t, 1, i - 1], ag_r.at[t, 1, i - 1], along(i, False),
            )
            for i in range(1, 4)
        ]

    def first_copies(t):
        ref = gathered[t].at[c, first]
        return [
            remote(ref, ref, ag_s.at[t, 2, i - 1], ag_r.at[t, 2, i - 1], along(i, True))
            for i in range(1, 4)
        ]

    def came(i):
        return lax.rem(first + 4 - i, 4)

    def core_copy(t, i):
        ref = gathered[t].at[c, came(i)]
        return remote(
            ref, ref, ag_s.at[t, 3, i], ag_r.at[t, 3, i], (g, zh * 2 + 1 - c)
        )

    def gather_second(t):
        for k in range(3):
            wait_for(met[t].at[0], ag_r.at[t, 0, k])
        for chunk in range(2):
            for to_zh in range(2):
                summed[t][chunk * 2 + to_zh] = (
                    met[t][to_zh, chunk] + met[t][2 + to_zh, chunk]
                ).astype(BF)
        own_copy(t).start()
        for copy in second_copies(t):
            copy.start()

    def gather_first(t):
        own_copy(t).wait()
        for i in range(1, 4):
            wait_for(gathered[t].at[c, first, second], ag_r.at[t, 1, i - 1])
        for copy in first_copies(t):
            copy.start()
        core_copy(t, 0).start()

    def gather_core(t):
        for i in range(1, 4):
            wait_for(gathered[t].at[c, came(i)], ag_r.at[t, 2, i - 1])
            core_copy(t, i).start()

    def gather_end(t):
        for i in range(4):
            wait_for(gathered[t].at[1 - c, 0], ag_r.at[t, 3, i])

    def attend_back(u, qi, ki, masked):
        lane = lax.broadcasted_iota(jnp.int32, (256, 128), 1)
        for half in range(2):
            keys = pl.ds(half * 256, 256)
            first_q = 256 if masked and half == 1 else 0
            d_v, d_k = [], []
            for head in range(2):
                d_w = mm(vn[ki, keys, :], dom[qi, head, :, first_q:])
                d_s = (d_w * fc[u, head, keys, first_q:].astype(F32)).astype(BF)
                d_v.append(mm(wc[u, head, keys, first_q:], don[qi, first_q:, :]))
                d_k.append(mm(d_s, qn[qi, first_q:, :]))
                part = mm(act[ki, 384 + head * 64 : 448 + head * 64, keys], d_s)
                lanes = slice(head * 64, head * 64 + 64)
                if half == 0:
                    out_u[u, lanes, :] = part
                else:
                    out_u[u, lanes, first_q:] += part
            dv_u[u, keys, :] = jnp.where(lane < 64, d_v[0], d_v[1])
            dk_u[u, keys, :] = jnp.where(lane < 64, d_k[0], d_k[1])

    def finish(q):
        d_q, d_k, d_v = out_u[q], dk_u[q], dv_u[q]
        if q == 0:
            d_k = d_k + in_a * (dk_u[4] + dk_u[5])
            d_v = d_v + in_a * (dv_u[4] + dv_u[5])
        if q == 1:
            d_q = d_q + in_a * out_u[4]
            d_k = d_k + dk_u[6] + in_b * dk_u[5]
            d_v = d_v + dv_u[6] + in_b * dv_u[5]
        if q == 2:
            d_q = d_q + out_u[6] + in_a * out_u[5]
            d_k = d_k + in_b * dk_u[4]
            d_v = d_v + in_b * dv_u[4]
        if q == 3:
            d_q = d_q + in_b * (out_u[4] + out_u[5])
        dpre[q, 128:256, :] = (2.0 * d_v.T * slope[q, 128:256, :]).astype(BF)
        dpre[q, 256:384, :] = (0.125 * d_q * slope[q, 256:384, :]).astype(BF)
        dpre[q, 384:512, :] = (d_k.T * slope[q, 384:512, :]).astype(BF)

    def dx_core(k):
        return remote(
            dxs.at[k], dxp.at[k], dxc_s.at[k], dxc_r.at[k], (g, zh * 2 + 1 - c)
        )

    def to_partner(k):
        q = 3 * (1 - c) if k == 0 else 1 + c
        dxs[k] = mm(dpre[q], wt[...], TN).astype(BF)
        dx_core(k).start()

    def rows_of(zl_, h):
        return pl.ds(pl.multiple_of(zl_ * 256 + h * 128, 128), 128)

    def dx_across(k, h):
        to_zh = c if k == 0 else 1 - c
        code = jnp.where(to_zh == zh, 0, 1)
        return remote(
            dxs.at[2 + k, rows_of(1 - zl, h)], zr.at[code, h],
            dxz_s.at[code, h], dxz_r.at[code, h],
            (grp(x, 1 - zl, y), to_zh * 2 + c),
        )

    def dx_same(k, h):
        return remote(
            dxs.at[2 + k, rows_of(zl, h)], zr.at[2, h], dxz_s.at[2, h], dxz_r.at[2, h],
            (g, (1 - zh) * 2 + c),
        )

    def to_planes(k):
        q = 3 * c if k == 0 else 2 - c
        to_zh = c if k == 0 else 1 - c
        mine = mm(dpre[q], wt[...], TN)
        wait_for(dxp.at[k], dxc_r.at[k])
        both = (mine + dxp[k].astype(F32)).astype(BF)
        back = jnp.where(
            lax.broadcasted_iota(jnp.int32, (512, 512), 0) == slot_of(places[q]), 1.0, 0.0
        ).astype(BF)
        dxs[2 + k] = mm(back, both).astype(BF)

        for h in range(2):

            @pl.when(to_zh != zh)
            def _(h=h):
                dx_same(k, h).start()

            dx_across(k, h).start()

    @pl.loop(0, 2)
    def _(f):
        attend_back(4 + f, query_of(f), key_of(f), False)

    @pl.loop(0, 2)
    def _(i):
        attend_back(3 * i, 3 * i, 3 * i, True)

    finish(0)
    finish(3)
    to_partner(0)
    meet(0)
    for q in (0, 3):
        part = mm(dpre[q, 128:, :], x_all[q])
        if q == 0:
            acc[...] = part
        else:
            acc[...] += part
    to_planes(0)

    @pl.loop(1, 3)
    def _(q):
        attend_back(q, q, q, True)

    gather_second(0)
    attend_back(6, 2, 1, False)
    finish(1)
    finish(2)
    to_partner(1)
    total = acc[...] + mm(dpre[1, 128:, :], x_all[1]) + mm(dpre[2, 128:, :], x_all[2])
    for b in range(3):
        gl_s[:, :, :, b] = (
            total[b * 128 : (b + 1) * 128].T.astype(BF).reshape(4, 2, 4, 16, 128)
        )
    grads_out(gl_s, gl_r, gl_sem)
    to_planes(1)

    def go_home(h):
        for k in range(3):
            wait_for(zr.at[k, h], dxz_r.at[k, h])
        keep = jnp.where(c == zh, 2, 3)
        own = (dxs[keep, rows_of(zl, h)].astype(F32) + zr[2, h].astype(F32)).astype(BF)
        other = (zr[0, h].astype(F32) + zr[1, h].astype(F32)).astype(BF)
        fin[pl.ds(zl, 1), slots(h)] = own.reshape(1, 8, 16, 512)
        fin[pl.ds(1 - zl, 1), slots(h)] = other.reshape(1, 8, 16, 512)

        @pl.loop(1 - h, 8)
        def _(j):
            i = j + 8 * h
            tx, ty = shifted(i, -1)
            remote(
                fin.at[:, i], dx_out.at[x, :, y], home_sem.at[0], home_sem.at[1],
                (grp(tx, zl, ty), s),
            ).start()

        if h == 0:
            pltpu.make_async_copy(fin.at[:, 0], dx_out.at[x, :, y], home_sem.at[1]).start()

    meet(1)
    gather_first(0)
    gather_second(1)
    go_home(0)
    gather_first(1)
    go_home(1)
    gather_core(0)
    gather_core(1)
    gather_end(0)
    gather_end(1)

    wait_for(dx_out, home_sem.at[1])
    wait_for(fin.at[:, 0:15], home_sem.at[0])
    for t in range(2):
        for copy in z_copies(t) + second_copies(t) + first_copies(t):
            copy.wait_send()
        for i in range(4):
            core_copy(t, i).wait_send()
    for a in range(2):
        wait_for(rows.at[a, c, 0:2, 0, 0:15], plane_s.at[a])
        for h in range(2):
            for k in range(3):
                z_out(a, k, h).wait_send()
            for k in range(4):
                core_out(a, k, h).wait_send()
    for i in range(1, 4):
        wait_for(places.at[0], seq_s.at[0, i - 1])
        stats_out(i).wait_send()
    for k in range(2):
        dx_core(k).wait_send()
    for h in range(2):
        for k in range(3):
            wait_for(zr.at[k, h], dxz_s.at[k, h])
    wait_for(ge_r.at[0:15], ge_sem.at[0])
    wait_for(gl_r.at[0:15], gl_sem.at[0])


def finish_kernel(dx_ref, dy_ref, e0, e1, l0, l1, dx_out, gin_out, gout_out):
    factor = 1.0 / 256.0
    dx_out[...] = (dx_ref[...].astype(F32) + dy_ref[...].astype(F32)).astype(BF)
    for core in range(2):
        for y in range(4):
            for z in range(4):
                zl, position = z // 2, (z % 2) * 2 + core
                early = e0[0, 0, y, z] if core == 0 else e1[0, y, 0, z]
                late = l0[0, 0, y, z] if core == 0 else l1[0, y, 0, z]
                at = slice((zl * 4 + y) * 16, (zl * 4 + y) * 16 + 16)
                for b in range(4):
                    lo = b * 512 + position * 128
                    part = early[0] if b == 0 else late[b - 1]
                    gin_out[at, lo : lo + 128] = part.astype(F32) * factor
                lo = position * 128 + (zl * 4 + y) * 16
                gout_out[lo : lo + 16, :] = early[1].astype(F32) * factor


def per_device(x_home, dy_home, w_in, w_out, place, seg_ids):
    shape = (4, 2, 4, 16, 512)
    vm = pltpu.VMEM
    dma = pltpu.SemaphoreType.DMA
    hbm = pl.BlockSpec(memory_space=pl.ANY)
    in_vmem = pl.BlockSpec(memory_space=pltpu.VMEM)
    dx, early, late = pl.pallas_call(
        kernel,
        out_shape=(
            jax.ShapeDtypeStruct(shape, BF),
            jax.ShapeDtypeStruct((2, 4, 4, 4, 2, 16, 128), BF),
            jax.ShapeDtypeStruct((2, 4, 4, 4, 3, 16, 128), BF),
        ),
        in_specs=[
            hbm, hbm, hbm, hbm, in_vmem, pl.BlockSpec(memory_space=pltpu.SMEM),
        ],
        out_specs=(hbm, hbm, hbm),
        scratch_shapes=[
            vm((2, 2, 3, 2, 16, 16, 512), BF),
            vm((4, 512, 512), BF),
            vm((4, 512, 512), BF),
            vm((4, 512, 512), BF),
            vm((4, 512, 512), BF),
            vm((4, 512, 512), F32),
            vm((4, 2, 128, 512), BF),
            vm((4, 512, 128), BF),
            vm((4, 512, 128), BF),
            vm((4, 512, 128), BF),
            vm((7, 2, 512, 512), BF),
            vm((7, 2, 512, 512), BF),
            vm((7, 128, 512), F32),
            vm((4, 128, 512), F32),
            vm((4, 4, 4, 512), F32),
            vm((4, 2, 128, 512), BF),
            vm((4, 512, 128), BF),
            vm((7, 512, 128), F32),
            vm((7, 512, 128), F32),
            vm((4, 512, 512), BF),
            vm((512, 512), BF),
            vm((512, 512), BF),
            vm((128, 512), BF),
            vm((4, 1, 512), jnp.int32),
            vm((4, 2, 4, 2, 16, 128), BF),
            vm((16, 2, 2, 16, 128), BF),
            vm((4, 2, 4, 3, 16, 128), BF),
            vm((16, 2, 3, 16, 128), BF),
            vm((4, 2, 2, 16, 128), F32),
            vm((4, 2, 16, 128), BF),
            vm((4, 2, 3, 16, 128), F32),
            vm((4, 3, 16, 128), BF),
            vm((384, 512), F32),
            vm((4, 512, 512), BF),
            vm((2, 512, 512), BF),
            vm((3, 2, 128, 512), BF),
            vm((2, 16, 16, 512), BF),
            dma((6,)), dma((2,)), dma((2, 2)), dma((2, 3, 2)), dma((2, 3, 2)),
            dma((2, 4, 2)), dma((2, 4, 2)), dma((2, 3)), dma((2, 3)), dma((2,)), dma((2,)),
            dma((2, 4, 4)), dma((2, 4, 4)), dma((2,)), dma((2,)), dma((2,)),
            dma((3, 2)), dma((3, 2)), dma((2,)),
        ],
        compiler_params=pltpu.CompilerParams(
            collective_id=0, has_side_effects=True, vmem_limit_bytes=63 * 2**20
        ),
    )(
        x_home.reshape(shape),
        dy_home.reshape(shape),
        w_in,
        w_out,
        place.reshape(1, 512),
        seg_ids.reshape(1, 2048),
    )
    row = pl.BlockSpec((128, 512), lambda i: (i, 0))

    def part(core, blocks):
        if core == 0:
            return pl.BlockSpec((1, 1, 4, 4, blocks, 16, 128), lambda i: (0, i, 0, 0, 0, 0, 0))
        return pl.BlockSpec((1, 4, 1, 4, blocks, 16, 128), lambda i: (1, 0, i, 0, 0, 0, 0))

    return pl.pallas_call(
        finish_kernel,
        grid=(4,),
        out_shape=(
            jax.ShapeDtypeStruct((512, 512), BF),
            jax.ShapeDtypeStruct((512, 2048), F32),
            jax.ShapeDtypeStruct((512, 512), F32),
        ),
        in_specs=[row, row, part(0, 2), part(1, 2), part(0, 3), part(1, 3)],
        out_specs=(
            row,
            pl.BlockSpec((128, 2048), lambda i: (i, 0)),
            pl.BlockSpec((512, 128), lambda i: (0, i)),
        ),
    )(dx.reshape(512, 512), dy_home, early, early, late, late)


def solution(mesh):
    in_specs = (
        P(("grp", "seq"), None),
        P(("grp", "seq"), None),
        P(),
        P(),
        P("grp", "seq", None),
        P("grp", None),
    )
    out_specs = (P(("grp", "seq"), None), P(), P())
    return jax.shard_map(
        per_device, mesh=mesh, in_specs=in_specs, out_specs=out_specs, check_vma=False
    )
```

```python
import jax
import jax.numpy as jnp
from jax import lax
from jax.experimental import pallas as pl
from jax.experimental.pallas import tpu as pltpu
from jax.sharding import PartitionSpec as P

BF = jnp.bfloat16
F32 = jnp.float32
MESH = pl.DeviceIdType.MESH
NN = (((1,), (0,)), ((), ()))
NT = (((1,), (1,)), ((), ()))
TN = (((0,), (0,)), ((), ()))


def mm(a, b, dims=NN):
    return lax.dot_general(a, b, dims, preferred_element_type=F32)


def remote(src, dst, send, recv, device):
    return pltpu.make_async_remote_copy(
        src_ref=src,
        dst_ref=dst,
        send_sem=send,
        recv_sem=recv,
        device_id=device,
        device_id_type=MESH,
    )


def wait_for(ref, sem):
    pltpu.make_async_copy(ref, ref, sem).wait()


def kernel(
    x_ref, dy_ref, win_ref, wout_ref, place_ref, seg_ref,
    dx_out, age, agl,
    rows, perm, x_all, dy_all, act, slope, qm, qn, kn, vn, wc, fc, out_u, out_t, dm_t, stats,
    dom, don, dv_u, dk_u, dpre, wsl, wt, wo, places,
    ge_s, ge_r, gl_s, gl_r, met_e, mine_e, met_l, mine_l, acc, dxs, dxp, zr, fin,
    local_sem, plane_s, plane_r, z_s, z_r, core_s, core_r, seq_s, seq_r, ge_sem, gl_sem,
    ag_s, ag_r, ag_l, first_r, other_r, dxc_s, dxc_r, dxz_s, dxz_r, home_sem,
):
    g = lax.axis_index("grp")
    s = lax.axis_index("seq")
    x, zl, y = g // 8, (g // 4) % 2, g % 4
    zh, c = s // 2, s % 2

    def grp(x_, zl_, y_):
        return (x_ * 2 + zl_) * 4 + y_

    weight_copies = []
    for b in range(4):
        weight_copies.append(
            pltpu.make_async_copy(
                win_ref.at[:, pl.ds(pl.multiple_of(b * 512 + s * 128, 128), 128)],
                wsl.at[:, b * 128 : (b + 1) * 128],
                local_sem.at[b],
            )
        )
    weight_copies.append(
        pltpu.make_async_copy(
            wout_ref.at[pl.ds(pl.multiple_of(s * 128, 128), 128)], wo, local_sem.at[4]
        )
    )
    for copy in weight_copies:
        copy.start()

    barrier = pltpu.get_barrier_semaphore()

    def shifted(i, sign):
        return lax.rem(x + 4 + sign * (i // 4), 4), lax.rem(y + 4 + sign * lax.rem(i, 4), 4)

    @pl.loop(1, 16)
    def _(i):
        tx, ty = shifted(i, 1)
        pl.semaphore_signal(
            barrier, inc=1, device_id=(grp(tx, zl, ty), s), device_id_type=MESH
        )

    for i in range(1, 4):
        pl.semaphore_signal(
            barrier, inc=1, device_id=(g, lax.rem(s + i, 4)), device_id_type=MESH
        )
    for to_zh in range(2):
        pl.semaphore_signal(
            barrier, inc=1, device_id=(grp(x, 1 - zl, y), to_zh * 2 + c), device_id_type=MESH
        )
    pl.semaphore_wait(barrier, 20)

    homes = (x_ref, dy_ref)
    for a in range(2):
        for h in range(2):

            @pl.loop(1 - h, 8)
            def _(j, a=a, h=h):
                i = j + 8 * h
                tx, ty = shifted(i, 1)
                remote(
                    homes[a].at[tx, :, ty],
                    rows.at[a, c, pl.ds(zl, 2), zh, i],
                    plane_s.at[a],
                    plane_r.at[a, h],
                    (grp(tx, zl, ty), s),
                ).start()

            if h == 0:
                pltpu.make_async_copy(
                    homes[a].at[x, :, y], rows.at[a, c, pl.ds(zl, 2), zh, 0], plane_r.at[a, 0]
                ).start()
        if a == 0:
            pltpu.make_async_copy(place_ref, places.at[s], local_sem.at[5]).start()
            for i in range(1, 4):
                remote(
                    place_ref,
                    places.at[s],
                    seq_s.at[0],
                    seq_r.at[0, i - 1],
                    (g, lax.rem(s + i, 4)),
                ).start()

    z_peers = (
        (grp(x, 1 - zl, y), s),
        (grp(x, 1 - zl, y), (1 - zh) * 2 + c),
        (g, (1 - zh) * 2 + c),
    )

    def slots(h):
        return slice(8 * h, 8 * h + 8)

    def block(a, core, zl_, zh_, h):
        return rows.at[a, core, 2 * zl_, zh_, slots(h)]

    def z_out(a, k, h):
        src = rows.at[a, c, 1, zh, slots(h)] if k < 2 else block(a, c, zl, zh, h)
        return remote(
            src, block(a, c, zl, zh, h), z_s.at[a], z_r.at[a, k, h], z_peers[k]
        )

    where_from = ((1 - zl, zh), (1 - zl, 1 - zh), (zl, 1 - zh), (zl, zh))

    def core_out(a, k, h):
        ref = block(a, c, *where_from[k], h)
        return remote(
            ref, ref, core_s.at[a], core_r.at[a, k, h], (g, zh * 2 + 1 - c)
        )

    def spread_plane(a, h):
        wait_for(rows.at[a, c, pl.ds(zl, 2), zh, slots(h)], plane_r.at[a, h])
        for k in range(3):
            z_out(a, k, h).start()
        core_out(a, 3, h).start()

    def forward(a, k, h):
        wait_for(block(a, c, *where_from[k], h), z_r.at[a, k, h])
        core_out(a, k, h).start()

    def from_core(a, k):
        for h in range(2):
            wait_for(block(a, 1 - c, *where_from[k], h), core_r.at[a, k, h])

    for copy in weight_copies:
        copy.wait()
    wt[...] = wsl[...].T
    spread_plane(0, 0)
    spread_plane(0, 1)

    wait_for(places.at[0], local_sem.at[5])
    for i in range(1, 4):
        wait_for(places.at[0], seq_r.at[0, i - 1])

    def slot_of(p):
        apart = ((x - (p >> 7)) & 3) * 4 + ((y - (p >> 4)) & 3)
        return ((p >> 6) & 1) * 256 + apart * 16 + (p & 15)

    @pl.loop(0, 4)
    def _(q):
        slot = slot_of(places[q])
        column = jnp.broadcast_to(slot.astype(F32), (128, 512)).T
        lane = lax.broadcasted_iota(jnp.int32, (512, 128), 1).astype(F32)
        for b in range(4):
            perm[q, :, b * 128 : (b + 1) * 128] = jnp.where(
                column == lane + float(b * 128), 1.0, 0.0
            ).astype(BF)

    def ordered(a, q):
        low = rows[a, lax.rem(q, 2), 0, q // 2].reshape(256, 512)
        high = rows[a, lax.rem(q, 2), 2, q // 2].reshape(256, 512)
        return (mm(perm[q, :, :256], low) + mm(perm[q, :, 256:], high)).astype(BF)

    def project(q):
        x_all[q] = ordered(0, q)
        for b in range(4):
            pre = mm(wt[b * 128 : (b + 1) * 128, :], x_all[q], NT)
            sig = 0.5 * jnp.tanh(0.5 * pre) + 0.5
            full = pre * sig
            slope[q, b * 128 : (b + 1) * 128, :] = sig + full * (1.0 - sig)
            cut = full.astype(BF)
            act[q, b * 128 : (b + 1) * 128, :] = cut
            if b == 1:
                vn[q] = cut.T
            if b == 2:
                qn[q] = (cut * BF(0.125)).T
                scaled = cut * BF(0.0625)
                zero = jnp.zeros((64, 512), BF)
                qm[q, 0] = jnp.concatenate([scaled[:64], zero], axis=0)
                qm[q, 1] = jnp.concatenate([zero, scaled[64:]], axis=0)
            if b == 3:
                kn[q] = cut.T

    is_a = seg_ref[0, 0] == seg_ref[0, 1535]
    in_a = jnp.where(is_a, 1.0, 0.0).astype(F32)
    in_b = 1.0 - in_a
    long, short = 1.0 / 1536.0, 1.0 / 512.0
    inv_len = (
        in_a * long + in_b * short, long, long, in_a * short + in_b * long
    )

    def query_of(f):
        return jnp.where(f == 2, 2, jnp.where(is_a, f + 1, 3))

    def key_of(f):
        return jnp.where(f == 2, 1, jnp.where(is_a, 0, 2 - f))

    def causal(rows_, cols):
        return lax.broadcasted_iota(jnp.int32, (rows_, cols), 0) <= lax.broadcasted_iota(
            jnp.int32, (rows_, cols), 1
        )

    def weigh(u, qi, ki, head, half, first, masked):
        keys = pl.ds(half * 256, 256)
        h = mm(kn[ki, keys, :], qm[qi, head, :, first:])
        t = jnp.tanh(h)
        a = 1.0 + t
        w = h * a
        f = a * (1.0 - w) + (w + w)
        if masked:
            keep = causal(256, 512 - first)
            w = jnp.where(keep, w, 0.0)
            f = jnp.where(keep, f, 0.0)
        w = w.astype(BF)
        wc[u, head, keys, first:] = w
        fc[u, head, keys, first:] = f.astype(BF)
        return mm(act[ki, 128 + head * 64 : 192 + head * 64, keys], w)

    def diagonal(q):
        for head in range(2):
            lanes = slice(head * 64, head * 64 + 64)
            out_u[q, lanes, :] = weigh(q, q, q, head, 0, 0, True)
            out_u[q, lanes, 256:] += weigh(q, q, q, head, 1, 256, True)

    forward(0, 0, 0)
    forward(0, 0, 1)
    spread_plane(1, 0)
    forward(0, 1, 0)
    forward(0, 2, 0)
    spread_plane(1, 1)
    from_core(0, 3)
    from_core(0, 0)

    @pl.loop(0, 2)
    def _(j):
        project(zh * 2 + j)

    forward(0, 1, 1)
    forward(0, 2, 1)

    @pl.loop(0, 2)
    def _(j):
        diagonal(zh * 2 + j)

    from_core(0, 1)
    from_core(0, 2)

    @pl.loop(0, 2)
    def _(j):
        project((1 - zh) * 2 + j)

    forward(1, 0, 0)
    forward(1, 0, 1)

    @pl.loop(0, 2)
    def _(j):
        diagonal((1 - zh) * 2 + j)

    def across(f):
        qi, ki = query_of(f), key_of(f)
        for head in range(2):
            lanes = slice(head * 64, head * 64 + 64)
            out_u[4 + f, lanes, :] = weigh(4 + f, qi, ki, head, 0, 0, False) + weigh(
                4 + f, qi, ki, head, 1, 0, False
            )

    @pl.loop(0, 2)
    def _(f):
        across(f)

    for k in (1, 2):
        forward(1, k, 0)
    across(2)

    def sums(q):
        dy_all[q] = ordered(1, q)
        d_mixed = mm(wo[...], dy_all[q], NT)
        dm_t[q] = d_mixed
        with_4 = jnp.where(q == 1, in_a, jnp.where(q == 3, in_b, 0.0))
        with_5 = jnp.where(q == 2, in_a, jnp.where(q == 3, in_b, 0.0))
        with_6 = jnp.where(q == 2, 1.0, 0.0)
        total = out_u[q] + with_4 * out_u[4] + with_5 * out_u[5] + with_6 * out_u[6]
        total = total * jnp.where(q == 0, inv_len[0], jnp.where(q == 3, inv_len[3], long))
        out_t[q] = total
        centre = jnp.mean(total, axis=0, keepdims=True)
        away = total - centre
        d_normed = d_mixed * act[q, :128, :].astype(F32)
        stats[s, q, 0:1, :] = centre
        stats[s, q, 1:2, :] = jnp.sum(away * away, axis=0, keepdims=True)
        stats[s, q, 2:3, :] = jnp.sum(d_normed, axis=0, keepdims=True)
        stats[s, q, 3:4, :] = jnp.sum(d_normed * away, axis=0, keepdims=True)

    from_core(1, 3)
    from_core(1, 0)

    @pl.loop(0, 2)
    def _(j):
        sums(zh * 2 + j)

    for k in (1, 2):
        forward(1, k, 1)
    from_core(1, 1)
    from_core(1, 2)

    @pl.loop(0, 2)
    def _(j):
        sums((1 - zh) * 2 + j)

    def stats_out(i):
        return remote(
            stats.at[s], stats.at[s], seq_s.at[1], seq_r.at[1, i - 1],
            (g, lax.rem(s + i, 4)),
        )

    for i in range(1, 4):
        stats_out(i).start()
    for i in range(1, 4):
        wait_for(stats.at[lax.rem(s + i, 4)], seq_r.at[1, 3 - i])

    centres = [stats[r, :, 0, :] for r in range(4)]
    mean_all = (centres[0] + centres[1] + centres[2] + centres[3]) * 0.25
    square = jnp.zeros_like(mean_all)
    plain = jnp.zeros_like(mean_all)
    cross = jnp.zeros_like(mean_all)
    for r in range(4):
        off = centres[r] - mean_all
        square += stats[r, :, 1, :] + 128.0 * off * off
        plain += stats[r, :, 2, :]
        cross += stats[r, :, 3, :] + off * stats[r, :, 2, :]
    spread_all = lax.rsqrt(square * (1.0 / 512.0) + 1e-5)
    plain = plain * (1.0 / 512.0)
    cross = cross * spread_all * (1.0 / 512.0)

    grad_out = jnp.zeros((128, 512), F32)
    grad_u = jnp.zeros((128, 512), F32)
    for q in range(4):
        gate = act[q, :128, :].astype(F32)
        spread = spread_all[q : q + 1]
        normed = (out_t[q] - mean_all[q : q + 1]) * spread
        d_mixed = dm_t[q]
        mixed = (normed * gate).astype(BF)
        d_u = (d_mixed * normed * slope[q, :128, :]).astype(BF)
        dpre[q, :128, :] = d_u
        d_out = (
            (d_mixed * gate - plain[q : q + 1] - normed * cross[q : q + 1])
            * (spread * (0.5 * inv_len[q]))
        ).astype(BF)
        zero = jnp.zeros((64, 512), BF)
        dom[q, 0] = jnp.concatenate([d_out[:64], zero], axis=0)
        dom[q, 1] = jnp.concatenate([zero, d_out[64:]], axis=0)
        don[q] = d_out.T
        grad_out += mm(mixed, dy_all[q])
        grad_u += mm(d_u, x_all[q])

    def grads_out(buf, got, sem):
        @pl.loop(1, 16)
        def _(i):
            tx, ty = shifted(i, 1)
            remote(
                buf.at[tx, :, ty], got.at[i], sem.at[0], sem.at[1], (grp(tx, zl, ty), s)
            ).start()

        pltpu.make_async_copy(buf.at[x, :, y], got.at[0], sem.at[1]).start()

    ge_s[:, :, :, 0] = grad_u.T.astype(BF).reshape(4, 2, 4, 16, 128)
    for b in range(4):
        ge_s[b, :, :, 1] = (
            grad_out[:, b * 128 : (b + 1) * 128].astype(BF).reshape(2, 4, 16, 128)
        )
    grads_out(ge_s, ge_r, ge_sem)

    first = jnp.where(c == 0, x, y)
    second = jnp.where(c == 0, y, x)
    zz = zl * 2 + zh
    reduced = ((ge_r, ge_sem), (gl_r, gl_sem))
    met = (met_e, met_l)
    summed = (mine_e, mine_l)
    gathered = (age, agl)

    def z_copies(t):
        ref = met[t].at[zz]
        return [
            remote(ref, ref, ag_s.at[t, 0], ag_r.at[t, 0, k], peer)
            for k, peer in enumerate(z_peers)
        ]

    def meet(t):
        got, sem = reduced[t]
        wait_for(got, sem.at[1])
        met[t][zz] = jnp.sum(got[...].astype(F32), axis=0)
        for copy in z_copies(t):
            copy.start()

    def along(i, on_first):
        nf = lax.rem(first + i, 4) if on_first else first
        ns = second if on_first else lax.rem(second + i, 4)
        nx = jnp.where(c == 0, nf, ns)
        ny = jnp.where(c == 0, ns, nf)
        return (grp(nx, zl, ny), s)

    def piece(t, i, j):
        return gathered[t].at[
            c, lax.rem(first + 4 - j, 4), lax.rem(second + 4 - i, 4)
        ]

    def held(t, i):
        return summed[t] if i == 0 else piece(t, i, 0)

    def own_copy(t):
        return pltpu.make_async_copy(summed[t], piece(t, 0, 0), ag_l.at[t])

    def second_copies(t):
        return [
            remote(
                summed[t], piece(t, 0, 0),
                ag_s.at[t, 1], ag_r.at[t, 1, i - 1], along(i, False),
            )
            for i in range(1, 4)
        ]

    def first_copies(t, i):
        return [
            remote(
                held(t, i), piece(t, i, 0),
                ag_s.at[t, 2], first_r.at[t, i, j - 1], along(j, True),
            )
            for j in range(1, 4)
        ]

    def core_copy(t, i, j):
        return remote(
            held(t, i) if j == 0 else piece(t, i, j), piece(t, i, j),
            ag_s.at[t, 3], other_r.at[t], (g, zh * 2 + 1 - c),
        )

    def gather_start(t):
        for k in range(3):
            wait_for(met[t].at[0], ag_r.at[t, 0, k])
        for chunk in range(2):
            for to_zh in range(2):
                summed[t][chunk * 2 + to_zh] = (
                    met[t][to_zh, chunk] + met[t][2 + to_zh, chunk]
                ).astype(BF)
        for copy in second_copies(t) + first_copies(t, 0):
            copy.start()
        core_copy(t, 0, 0).start()
        own_copy(t).start()

    def gather_pass(t):
        for i in range(1, 4):
            wait_for(piece(t, i, 0), ag_r.at[t, 1, i - 1])
            for copy in first_copies(t, i):
                copy.start()
            core_copy(t, i, 0).start()

    def gather_core(t):
        for i in range(4):
            for j in range(1, 4):
                wait_for(piece(t, i, j), first_r.at[t, i, j - 1])
                core_copy(t, i, j).start()

    def gather_end(t):
        own_copy(t).wait()
        wait_for(gathered[t].at[1 - c], other_r.at[t])

    def attend_back(u, qi, ki, masked):
        lane = lax.broadcasted_iota(jnp.int32, (256, 128), 1)
        for half in range(2):
            keys = pl.ds(half * 256, 256)
            first_q = 256 if masked and half == 1 else 0
            d_v, d_k = [], []
            for head in range(2):
                d_w = mm(vn[ki, keys, :], dom[qi, head, :, first_q:])
                d_s = (d_w * fc[u, head, keys, first_q:].astype(F32)).astype(BF)
                d_v.append(mm(wc[u, head, keys, first_q:], don[qi, first_q:, :]))
                d_k.append(mm(d_s, qn[qi, first_q:, :]))
                part = mm(act[ki, 384 + head * 64 : 448 + head * 64, keys], d_s)
                lanes = slice(head * 64, head * 64 + 64)
                if half == 0:
                    out_u[u, lanes, :] = part
                else:
                    out_u[u, lanes, first_q:] += part
            dv_u[u, keys, :] = jnp.where(lane < 64, d_v[0], d_v[1])
            dk_u[u, keys, :] = jnp.where(lane < 64, d_k[0], d_k[1])

    def finish(q):
        d_q, d_k, d_v = out_u[q], dk_u[q], dv_u[q]
        if q == 0:
            d_k = d_k + in_a * (dk_u[4] + dk_u[5])
            d_v = d_v + in_a * (dv_u[4] + dv_u[5])
        if q == 1:
            d_q = d_q + in_a * out_u[4]
            d_k = d_k + dk_u[6] + in_b * dk_u[5]
            d_v = d_v + dv_u[6] + in_b * dv_u[5]
        if q == 2:
            d_q = d_q + out_u[6] + in_a * out_u[5]
            d_k = d_k + in_b * dk_u[4]
            d_v = d_v + in_b * dv_u[4]
        if q == 3:
            d_q = d_q + in_b * (out_u[4] + out_u[5])
        dpre[q, 128:256, :] = (2.0 * d_v.T * slope[q, 128:256, :]).astype(BF)
        dpre[q, 256:384, :] = (0.125 * d_q * slope[q, 256:384, :]).astype(BF)
        dpre[q, 384:512, :] = (d_k.T * slope[q, 384:512, :]).astype(BF)

    def dx_core(k):
        return remote(
            dxs.at[k], dxp.at[k], dxc_s.at[0], dxc_r.at[k], (g, zh * 2 + 1 - c)
        )

    def to_partner(k):
        q = 3 * (1 - c) if k == 0 else 1 + c
        dxs[k] = mm(dpre[q], wt[...], TN).astype(BF)
        dx_core(k).start()

    def rows_of(zl_, h):
        return pl.ds(pl.multiple_of(zl_ * 256 + h * 128, 128), 128)

    def dx_across(k, h):
        to_zh = c if k == 0 else 1 - c
        code = jnp.where(to_zh == zh, 0, 1)
        return remote(
            dxs.at[2 + k, rows_of(1 - zl, h)], zr.at[code, h],
            dxz_s.at[0], dxz_r.at[code, h],
            (grp(x, 1 - zl, y), to_zh * 2 + c),
        )

    def dx_same(k, h):
        return remote(
            dxs.at[2 + k, rows_of(zl, h)], zr.at[2, h], dxz_s.at[0], dxz_r.at[2, h],
            (g, (1 - zh) * 2 + c),
        )

    def to_planes(k):
        q = 3 * c if k == 0 else 2 - c
        to_zh = c if k == 0 else 1 - c
        mine = mm(dpre[q], wt[...], TN)
        wait_for(dxp.at[k], dxc_r.at[k])
        both = (mine + dxp[k].astype(F32)).astype(BF)
        back = jnp.where(
            lax.broadcasted_iota(jnp.int32, (512, 512), 0) == slot_of(places[q]), 1.0, 0.0
        ).astype(BF)
        dxs[2 + k] = mm(back, both).astype(BF)

        for h in range(2):

            @pl.when(to_zh != zh)
            def _(h=h):
                dx_same(k, h).start()

            dx_across(k, h).start()

    @pl.loop(0, 2)
    def _(f):
        attend_back(4 + f, query_of(f), key_of(f), False)

    @pl.loop(0, 2)
    def _(i):
        attend_back(3 * i, 3 * i, 3 * i, True)

    finish(0)
    finish(3)
    to_partner(0)
    meet(0)
    for q in (0, 3):
        part = mm(dpre[q, 128:, :], x_all[q])
        if q == 0:
            acc[...] = part
        else:
            acc[...] += part
    to_planes(0)

    @pl.loop(1, 3)
    def _(q):
        attend_back(q, q, q, True)

    gather_start(0)
    attend_back(6, 2, 1, False)
    finish(1)
    finish(2)
    to_partner(1)
    total = acc[...] + mm(dpre[1, 128:, :], x_all[1]) + mm(dpre[2, 128:, :], x_all[2])
    for b in range(3):
        gl_s[:, :, :, b] = (
            total[b * 128 : (b + 1) * 128].T.astype(BF).reshape(4, 2, 4, 16, 128)
        )
    grads_out(gl_s, gl_r, gl_sem)
    to_planes(1)

    def go_home(h):
        for k in range(3):
            wait_for(zr.at[k, h], dxz_r.at[k, h])
        keep = jnp.where(c == zh, 2, 3)
        own = (dxs[keep, rows_of(zl, h)].astype(F32) + zr[2, h].astype(F32)).astype(BF)
        other = (zr[0, h].astype(F32) + zr[1, h].astype(F32)).astype(BF)
        fin[pl.ds(zl, 1), slots(h)] = own.reshape(1, 8, 16, 512)
        fin[pl.ds(1 - zl, 1), slots(h)] = other.reshape(1, 8, 16, 512)

        @pl.loop(1 - h, 8)
        def _(j):
            i = j + 8 * h
            tx, ty = shifted(i, -1)
            remote(
                fin.at[:, i], dx_out.at[x, :, y], home_sem.at[0], home_sem.at[1],
                (grp(tx, zl, ty), s),
            ).start()

        if h == 0:
            pltpu.make_async_copy(fin.at[:, 0], dx_out.at[x, :, y], home_sem.at[1]).start()

    for a in range(2):
        wait_for(rows.at[a, c, 0:2, 0, 0:15], plane_s.at[a])
        wait_for(rows.at[a, c, :, 0], z_s.at[a])
        wait_for(rows.at[a, c, 0:2], core_s.at[a])
    wait_for(places.at[0:3], seq_s.at[0])
    wait_for(stats.at[0:3], seq_s.at[1])
    wait_for(dxs.at[0:2], dxc_s.at[0])
    wait_for(ge_r.at[0:15], ge_sem.at[0])
    meet(1)
    wait_for(gl_r.at[0:15], gl_sem.at[0])
    gather_pass(0)
    gather_start(1)
    gather_pass(1)
    go_home(0)
    go_home(1)
    gather_core(0)
    gather_core(1)
    gather_end(0)
    gather_end(1)

    wait_for(dx_out, home_sem.at[1])
    wait_for(fin.at[:, 0:15], home_sem.at[0])
    wait_for(zr, dxz_s.at[0])
    for t in range(2):
        wait_for(met[t].at[0:3], ag_s.at[t, 0])
        wait_for(gathered[t].at[0, 0, 0:3], ag_s.at[t, 1])
        wait_for(gathered[t].at[0, 0:3], ag_s.at[t, 2])
        wait_for(gathered[t].at[0], ag_s.at[t, 3])


def finish_kernel(dx_ref, dy_ref, e_ref, l_ref, dx_out, gin_out, gout_out, e, l, dxv, dyv, gin, gout, sem, out_sem):
    factor = 1.0 / 256.0
    loads = []
    for core, axis in ((1, 0), (1, 1), (1, 2), (1, 3), (0, 0), (0, 1), (0, 2), (0, 3)):
        k = len(loads)
        loads.append(
            (
                pltpu.make_async_copy(e_ref.at[core, axis], e.at[core, axis], sem.at[0, k]),
                pltpu.make_async_copy(l_ref.at[core, axis], l.at[core, axis], sem.at[1, k]),
            )
        )
        for copy in loads[-1]:
            copy.start()
    rows_in = (
        pltpu.make_async_copy(dx_ref, dxv, sem.at[0, 8]),
        pltpu.make_async_copy(dy_ref, dyv, sem.at[1, 8]),
    )
    for copy in rows_in:
        copy.start()
    for pair in loads[:4]:
        for copy in pair:
            copy.wait()
    stores = []
    for x in range(4):
        for copy in loads[4 + x]:
            copy.wait()
        for core in range(2):
            for y in range(4):
                for z in range(4):
                    position = (z % 2) * 2 + core
                    at = (core, x, y, z) if core == 0 else (core, y, x, z)
                    row = x * 128 + (z // 2) * 64 + y * 16
                    for b in range(4):
                        tile = e[*at, 0] if b == 0 else l[*at, b - 1]
                        lo = b * 512 + position * 128
                        gin[row : row + 16, lo : lo + 128] = tile.astype(F32) * factor
                    row = position * 128 + (z // 2) * 64 + y * 16
                    gout[row : row + 16, x * 128 : x * 128 + 128] = (
                        e[*at, 1].astype(F32) * factor
                    )
        part = slice(x * 128, x * 128 + 128)
        stores.append(
            pltpu.make_async_copy(gin.at[part], gin_out.at[part], out_sem.at[x])
        )
        stores[-1].start()
    for x in range(2):
        part = slice(x * 256, x * 256 + 256)
        stores.append(
            pltpu.make_async_copy(gout.at[part], gout_out.at[part], out_sem.at[4 + x])
        )
        stores[-1].start()
    for copy in rows_in:
        copy.wait()
    dxv[...] = (dxv[...].astype(F32) + dyv[...].astype(F32)).astype(BF)
    stores.append(pltpu.make_async_copy(dxv, dx_out, out_sem.at[6]))
    stores[-1].start()
    for copy in stores:
        copy.wait()


def per_device(x_home, dy_home, w_in, w_out, place, seg_ids):
    shape = (4, 2, 4, 16, 512)
    vm = pltpu.VMEM
    dma = pltpu.SemaphoreType.DMA
    hbm = pl.BlockSpec(memory_space=pl.ANY)
    in_vmem = pl.BlockSpec(memory_space=pltpu.VMEM)
    dx, early, late = pl.pallas_call(
        kernel,
        out_shape=(
            jax.ShapeDtypeStruct(shape, BF),
            jax.ShapeDtypeStruct((2, 4, 4, 4, 2, 16, 128), BF),
            jax.ShapeDtypeStruct((2, 4, 4, 4, 3, 16, 128), BF),
        ),
        in_specs=[
            hbm, hbm, hbm, hbm, in_vmem, pl.BlockSpec(memory_space=pltpu.SMEM),
        ],
        out_specs=(hbm, hbm, hbm),
        scratch_shapes=[
            vm((2, 2, 3, 2, 16, 16, 512), BF),
            vm((4, 512, 512), BF),
            vm((4, 512, 512), BF),
            vm((4, 512, 512), BF),
            vm((4, 512, 512), BF),
            vm((4, 512, 512), F32),
            vm((4, 2, 128, 512), BF),
            vm((4, 512, 128), BF),
            vm((4, 512, 128), BF),
            vm((4, 512, 128), BF),
            vm((7, 2, 512, 512), BF),
            vm((7, 2, 512, 512), BF),
            vm((7, 128, 512), F32),
            vm((4, 128, 512), F32),
            vm((4, 128, 512), F32),
            vm((4, 4, 4, 512), F32),
            vm((4, 2, 128, 512), BF),
            vm((4, 512, 128), BF),
            vm((7, 512, 128), F32),
            vm((7, 512, 128), F32),
            vm((4, 512, 512), BF),
            vm((512, 512), BF),
            vm((512, 512), BF),
            vm((128, 512), BF),
            vm((4, 1, 512), jnp.int32),
            vm((4, 2, 4, 2, 16, 128), BF),
            vm((16, 2, 2, 16, 128), BF),
            vm((4, 2, 4, 3, 16, 128), BF),
            vm((16, 2, 3, 16, 128), BF),
            vm((4, 2, 2, 16, 128), F32),
            vm((4, 2, 16, 128), BF),
            vm((4, 2, 3, 16, 128), F32),
            vm((4, 3, 16, 128), BF),
            vm((384, 512), F32),
            vm((4, 512, 512), BF),
            vm((2, 512, 512), BF),
            vm((3, 2, 128, 512), BF),
            vm((2, 16, 16, 512), BF),
            dma((6,)), dma((2,)), dma((2, 2)), dma((2,)), dma((2, 3, 2)),
            dma((2,)), dma((2, 4, 2)), dma((2,)), dma((2, 3)), dma((2,)), dma((2,)),
            dma((2, 4)), dma((2, 2, 3)), dma((2,)), dma((2, 4, 3)), dma((2,)),
            dma((1,)), dma((2,)), dma((1,)), dma((3, 2)), dma((2,)),
        ],
        compiler_params=pltpu.CompilerParams(
            collective_id=0, has_side_effects=True, vmem_limit_bytes=63 * 2**20
        ),
    )(
        x_home.reshape(shape),
        dy_home.reshape(shape),
        w_in,
        w_out,
        place.reshape(1, 512),
        seg_ids.reshape(1, 2048),
    )
    return pl.pallas_call(
        finish_kernel,
        out_shape=(
            jax.ShapeDtypeStruct((512, 512), BF),
            jax.ShapeDtypeStruct((512, 2048), F32),
            jax.ShapeDtypeStruct((512, 512), F32),
        ),
        in_specs=[hbm, hbm, hbm, hbm],
        out_specs=(hbm, hbm, hbm),
        scratch_shapes=[
            vm((2, 4, 4, 4, 2, 16, 128), BF),
            vm((2, 4, 4, 4, 3, 16, 128), BF),
            vm((512, 512), BF),
            vm((512, 512), BF),
            vm((512, 2048), F32),
            vm((512, 512), F32),
            dma((2, 9)),
            dma((7,)),
        ],
        compiler_params=pltpu.CompilerParams(vmem_limit_bytes=62 * 2**20),
    )(dx.reshape(512, 512), dy_home, early, late)


def solution(mesh):
    in_specs = (
        P(("grp", "seq"), None),
        P(("grp", "seq"), None),
        P(),
        P(),
        P("grp", "seq", None),
        P("grp", None),
    )
    out_specs = (P(("grp", "seq"), None), P(), P())
    return jax.shard_map(
        per_device, mesh=mesh, in_specs=in_specs, out_specs=out_specs, check_vma=False
    )
```

```python
import jax
import jax.numpy as jnp
from jax import lax
from jax.experimental import pallas as pl
from jax.experimental.pallas import tpu as pltpu
from jax.sharding import PartitionSpec as P

BF = jnp.bfloat16
F32 = jnp.float32
MESH = pl.DeviceIdType.MESH
NN = (((1,), (0,)), ((), ()))
NT = (((1,), (1,)), ((), ()))
TN = (((0,), (0,)), ((), ()))


def mm(a, b, dims=NN):
    return lax.dot_general(a, b, dims, preferred_element_type=F32)


def remote(src, dst, send, recv, device):
    return pltpu.make_async_remote_copy(
        src_ref=src,
        dst_ref=dst,
        send_sem=send,
        recv_sem=recv,
        device_id=device,
        device_id_type=MESH,
    )


def wait_for(ref, sem):
    pltpu.make_async_copy(ref, ref, sem).wait()


def kernel(
    x_ref, dy_ref, win_ref, wout_ref, place_ref, seg_ref,
    dx_out, age, agl,
    rows, perm, x_all, dy_all, act, slope, qm, qn, kn, vn, wc, fc, out_u, out_t, dm_t, stats,
    dom, don, dv_u, dk_u, dpre, wsl, wt, wo, places,
    ge_s, ge_r, gl_s, gl_r, met_e, mine_e, met_l, mine_l, acc, dxs, dxp, zr, fin,
    local_sem, plane_s, plane_r, z_s, z_r, core_s, core_r, seq_s, seq_r, ge_sem, gl_sem,
    ag_s, ag_r, ag_l, first_r, other_r, dxc_s, dxc_r, dxz_s, dxz_r, home_sem,
):
    g = lax.axis_index("grp")
    s = lax.axis_index("seq")
    x, zl, y = g // 8, (g // 4) % 2, g % 4
    zh, c = s // 2, s % 2

    def grp(x_, zl_, y_):
        return (x_ * 2 + zl_) * 4 + y_

    weight_copies = []
    for b in range(4):
        weight_copies.append(
            pltpu.make_async_copy(
                win_ref.at[:, pl.ds(pl.multiple_of(b * 512 + s * 128, 128), 128)],
                wsl.at[:, b * 128 : (b + 1) * 128],
                local_sem.at[b],
            )
        )
    weight_copies.append(
        pltpu.make_async_copy(
            wout_ref.at[pl.ds(pl.multiple_of(s * 128, 128), 128)], wo, local_sem.at[4]
        )
    )
    for copy in weight_copies:
        copy.start()

    barrier = pltpu.get_barrier_semaphore()

    def shifted(i, sign):
        return lax.rem(x + 4 + sign * (i // 4), 4), lax.rem(y + 4 + sign * lax.rem(i, 4), 4)

    @pl.loop(1, 16)
    def _(i):
        tx, ty = shifted(i, 1)
        pl.semaphore_signal(
            barrier, inc=1, device_id=(grp(tx, zl, ty), s), device_id_type=MESH
        )

    for i in range(1, 4):
        pl.semaphore_signal(
            barrier, inc=1, device_id=(g, lax.rem(s + i, 4)), device_id_type=MESH
        )
    for to_zh in range(2):
        pl.semaphore_signal(
            barrier, inc=1, device_id=(grp(x, 1 - zl, y), to_zh * 2 + c), device_id_type=MESH
        )
    pl.semaphore_wait(barrier, 20)

    homes = (x_ref, dy_ref)
    for a in range(2):
        for h in range(2):

            @pl.loop(1 - h, 8)
            def _(j, a=a, h=h):
                i = j + 8 * h
                tx, ty = shifted(i, 1)
                remote(
                    homes[a].at[tx, :, ty],
                    rows.at[a, c, pl.ds(zl, 2), zh, i],
                    plane_s.at[a],
                    plane_r.at[a, h],
                    (grp(tx, zl, ty), s),
                ).start()

            if h == 0:
                pltpu.make_async_copy(
                    homes[a].at[x, :, y], rows.at[a, c, pl.ds(zl, 2), zh, 0], plane_r.at[a, 0]
                ).start()
        if a == 0:
            pltpu.make_async_copy(place_ref, places.at[s], local_sem.at[5]).start()
            for i in range(1, 4):
                remote(
                    place_ref,
                    places.at[s],
                    seq_s.at[0],
                    seq_r.at[0, i - 1],
                    (g, lax.rem(s + i, 4)),
                ).start()

    z_peers = (
        (grp(x, 1 - zl, y), s),
        (grp(x, 1 - zl, y), (1 - zh) * 2 + c),
        (g, (1 - zh) * 2 + c),
    )

    def slots(h):
        return slice(8 * h, 8 * h + 8)

    def block(a, core, zl_, zh_, h):
        return rows.at[a, core, 2 * zl_, zh_, slots(h)]

    def z_out(a, k, h):
        src = rows.at[a, c, 1, zh, slots(h)] if k < 2 else block(a, c, zl, zh, h)
        return remote(
            src, block(a, c, zl, zh, h), z_s.at[a], z_r.at[a, k, h], z_peers[k]
        )

    where_from = ((1 - zl, zh), (1 - zl, 1 - zh), (zl, 1 - zh), (zl, zh))

    def core_out(a, k, h):
        ref = block(a, c, *where_from[k], h)
        return remote(
            ref, ref, core_s.at[a], core_r.at[a, k, h], (g, zh * 2 + 1 - c)
        )

    def spread_plane(a, h):
        wait_for(rows.at[a, c, pl.ds(zl, 2), zh, slots(h)], plane_r.at[a, h])
        for k in range(3):
            z_out(a, k, h).start()
        core_out(a, 3, h).start()

    def forward(a, k, h):
        wait_for(block(a, c, *where_from[k], h), z_r.at[a, k, h])
        core_out(a, k, h).start()

    def from_core(a, k):
        for h in range(2):
            wait_for(block(a, 1 - c, *where_from[k], h), core_r.at[a, k, h])

    for copy in weight_copies:
        copy.wait()
    wt[...] = wsl[...].T
    spread_plane(0, 0)
    spread_plane(0, 1)

    wait_for(places.at[0], local_sem.at[5])
    for i in range(1, 4):
        wait_for(places.at[0], seq_r.at[0, i - 1])

    def slot_of(p):
        apart = ((x - (p >> 7)) & 3) * 4 + ((y - (p >> 4)) & 3)
        return ((p >> 6) & 1) * 256 + apart * 16 + (p & 15)

    @pl.loop(0, 4)
    def _(q):
        slot = slot_of(places[q])
        column = jnp.broadcast_to(slot.astype(F32), (128, 512)).T
        lane = lax.broadcasted_iota(jnp.int32, (512, 128), 1).astype(F32)
        for b in range(4):
            perm[q, :, b * 128 : (b + 1) * 128] = jnp.where(
                column == lane + float(b * 128), 1.0, 0.0
            ).astype(BF)

    def ordered(a, q):
        low = rows[a, lax.rem(q, 2), 0, q // 2].reshape(256, 512)
        high = rows[a, lax.rem(q, 2), 2, q // 2].reshape(256, 512)
        return (mm(perm[q, :, :256], low) + mm(perm[q, :, 256:], high)).astype(BF)

    def project(q):
        x_all[q] = ordered(0, q)
        for b in range(4):
            pre = mm(wt[b * 128 : (b + 1) * 128, :], x_all[q], NT)
            sig = 0.5 * jnp.tanh(0.5 * pre) + 0.5
            full = pre * sig
            slope[q, b * 128 : (b + 1) * 128, :] = sig + full * (1.0 - sig)
            cut = full.astype(BF)
            act[q, b * 128 : (b + 1) * 128, :] = cut
            if b == 1:
                vn[q] = cut.T
            if b == 2:
                qn[q] = (cut * BF(0.125)).T
                scaled = cut * BF(0.0625)
                zero = jnp.zeros((64, 512), BF)
                qm[q, 0] = jnp.concatenate([scaled[:64], zero], axis=0)
                qm[q, 1] = jnp.concatenate([zero, scaled[64:]], axis=0)
            if b == 3:
                kn[q] = cut.T

    is_a = seg_ref[0, 0] == seg_ref[0, 1535]
    in_a = jnp.where(is_a, 1.0, 0.0).astype(F32)
    in_b = 1.0 - in_a
    long, short = 1.0 / 1536.0, 1.0 / 512.0
    inv_len = (
        in_a * long + in_b * short, long, long, in_a * short + in_b * long
    )

    def query_of(f):
        return jnp.where(f == 2, 2, jnp.where(is_a, f + 1, 3))

    def key_of(f):
        return jnp.where(f == 2, 1, jnp.where(is_a, 0, 2 - f))

    def causal(rows_, cols):
        return lax.broadcasted_iota(jnp.int32, (rows_, cols), 0) <= lax.broadcasted_iota(
            jnp.int32, (rows_, cols), 1
        )

    def weigh(u, qi, ki, head, half, first, masked):
        keys = pl.ds(half * 256, 256)
        h = mm(kn[ki, keys, :], qm[qi, head, :, first:])
        t = jnp.tanh(h)
        a = 1.0 + t
        w = h * a
        f = a * (1.0 - w) + (w + w)
        if masked:
            keep = causal(256, 512 - first)
            w = jnp.where(keep, w, 0.0)
            f = jnp.where(keep, f, 0.0)
        w = w.astype(BF)
        wc[u, head, keys, first:] = w
        fc[u, head, keys, first:] = f.astype(BF)
        return mm(act[ki, 128 + head * 64 : 192 + head * 64, keys], w)

    def diagonal(q):
        for head in range(2):
            lanes = slice(head * 64, head * 64 + 64)
            out_u[q, lanes, :] = weigh(q, q, q, head, 0, 0, True)
            out_u[q, lanes, 256:] += weigh(q, q, q, head, 1, 256, True)

    forward(0, 0, 0)
    forward(0, 0, 1)
    spread_plane(1, 0)
    forward(0, 1, 0)
    forward(0, 2, 0)
    spread_plane(1, 1)
    from_core(0, 3)
    from_core(0, 0)

    @pl.loop(0, 2)
    def _(j):
        project(zh * 2 + j)

    forward(0, 1, 1)
    forward(0, 2, 1)

    @pl.loop(0, 2)
    def _(j):
        diagonal(zh * 2 + j)

    from_core(0, 1)
    from_core(0, 2)

    @pl.loop(0, 2)
    def _(j):
        project((1 - zh) * 2 + j)

    forward(1, 0, 0)
    forward(1, 0, 1)

    @pl.loop(0, 2)
    def _(j):
        diagonal((1 - zh) * 2 + j)

    def across(f):
        qi, ki = query_of(f), key_of(f)
        for head in range(2):
            lanes = slice(head * 64, head * 64 + 64)
            out_u[4 + f, lanes, :] = weigh(4 + f, qi, ki, head, 0, 0, False) + weigh(
                4 + f, qi, ki, head, 1, 0, False
            )

    @pl.loop(0, 2)
    def _(f):
        across(f)

    for k in (1, 2):
        forward(1, k, 0)
    across(2)

    def sums(q):
        dy_all[q] = ordered(1, q)
        d_mixed = mm(wo[...], dy_all[q], NT)
        dm_t[q] = d_mixed
        with_4 = jnp.where(q == 1, in_a, jnp.where(q == 3, in_b, 0.0))
        with_5 = jnp.where(q == 2, in_a, jnp.where(q == 3, in_b, 0.0))
        with_6 = jnp.where(q == 2, 1.0, 0.0)
        total = out_u[q] + with_4 * out_u[4] + with_5 * out_u[5] + with_6 * out_u[6]
        total = total * jnp.where(q == 0, inv_len[0], jnp.where(q == 3, inv_len[3], long))
        out_t[q] = total
        centre = jnp.mean(total, axis=0, keepdims=True)
        away = total - centre
        d_normed = d_mixed * act[q, :128, :].astype(F32)
        stats[s, q, 0:1, :] = centre
        stats[s, q, 1:2, :] = jnp.sum(away * away, axis=0, keepdims=True)
        stats[s, q, 2:3, :] = jnp.sum(d_normed, axis=0, keepdims=True)
        stats[s, q, 3:4, :] = jnp.sum(d_normed * away, axis=0, keepdims=True)

    from_core(1, 3)
    from_core(1, 0)

    @pl.loop(0, 2)
    def _(j):
        sums(zh * 2 + j)

    for k in (1, 2):
        forward(1, k, 1)
    from_core(1, 1)
    from_core(1, 2)

    @pl.loop(0, 2)
    def _(j):
        sums((1 - zh) * 2 + j)

    def stats_out(i):
        return remote(
            stats.at[s], stats.at[s], seq_s.at[1], seq_r.at[1, i - 1],
            (g, lax.rem(s + i, 4)),
        )

    for i in range(1, 4):
        stats_out(i).start()
    for i in range(1, 4):
        wait_for(stats.at[lax.rem(s + i, 4)], seq_r.at[1, 3 - i])

    centres = [stats[r, :, 0, :] for r in range(4)]
    mean_all = (centres[0] + centres[1] + centres[2] + centres[3]) * 0.25
    square = jnp.zeros_like(mean_all)
    plain = jnp.zeros_like(mean_all)
    cross = jnp.zeros_like(mean_all)
    for r in range(4):
        off = centres[r] - mean_all
        square += stats[r, :, 1, :] + 128.0 * off * off
        plain += stats[r, :, 2, :]
        cross += stats[r, :, 3, :] + off * stats[r, :, 2, :]
    spread_all = lax.rsqrt(square * (1.0 / 512.0) + 1e-5)
    plain = plain * (1.0 / 512.0)
    cross = cross * spread_all * (1.0 / 512.0)

    grad_out = jnp.zeros((128, 512), F32)
    grad_u = jnp.zeros((128, 512), F32)
    for q in range(4):
        gate = act[q, :128, :].astype(F32)
        spread = spread_all[q : q + 1]
        normed = (out_t[q] - mean_all[q : q + 1]) * spread
        d_mixed = dm_t[q]
        mixed = (normed * gate).astype(BF)
        d_u = (d_mixed * normed * slope[q, :128, :]).astype(BF)
        dpre[q, :128, :] = d_u
        d_out = (
            (d_mixed * gate - plain[q : q + 1] - normed * cross[q : q + 1])
            * (spread * (0.5 * inv_len[q]))
        ).astype(BF)
        zero = jnp.zeros((64, 512), BF)
        dom[q, 0] = jnp.concatenate([d_out[:64], zero], axis=0)
        dom[q, 1] = jnp.concatenate([zero, d_out[64:]], axis=0)
        don[q] = d_out.T
        grad_out += mm(mixed, dy_all[q])
        grad_u += mm(d_u, x_all[q])

    def grads_out(buf, got, sem):
        for low, high in ((8, 16), (1, 8)):

            @pl.loop(low, high)
            def _(i):
                tx, ty = shifted(i, 1)
                remote(
                    buf.at[tx, :, ty], got.at[i], sem.at[0], sem.at[1],
                    (grp(tx, zl, ty), s),
                ).start()

        pltpu.make_async_copy(buf.at[x, :, y], got.at[0], sem.at[1]).start()

    ge_s[:, :, :, 0] = grad_u.T.astype(BF).reshape(4, 2, 4, 16, 128)
    for b in range(4):
        ge_s[b, :, :, 1] = (
            grad_out[:, b * 128 : (b + 1) * 128].astype(BF).reshape(2, 4, 16, 128)
        )
    grads_out(ge_s, ge_r, ge_sem)

    first = jnp.where(c == 0, x, y)
    second = jnp.where(c == 0, y, x)
    zz = zl * 2 + zh
    reduced = ((ge_r, ge_sem), (gl_r, gl_sem))
    met = (met_e, met_l)
    summed = (mine_e, mine_l)
    gathered = (age, agl)

    def z_copies(t):
        ref = met[t].at[zz]
        return [
            remote(ref, ref, ag_s.at[t, 0], ag_r.at[t, 0, k], peer)
            for k, peer in enumerate(z_peers)
        ]

    def meet(t):
        got, sem = reduced[t]
        wait_for(got, sem.at[1])
        met[t][zz] = jnp.sum(got[...].astype(F32), axis=0)
        for copy in z_copies(t):
            copy.start()

    def along(i, on_first):
        nf = lax.rem(first + i, 4) if on_first else first
        ns = second if on_first else lax.rem(second + i, 4)
        nx = jnp.where(c == 0, nf, ns)
        ny = jnp.where(c == 0, ns, nf)
        return (grp(nx, zl, ny), s)

    def piece(t, i, j):
        return gathered[t].at[
            c, lax.rem(first + 4 - j, 4), lax.rem(second + 4 - i, 4)
        ]

    def held(t, i):
        return summed[t] if i == 0 else piece(t, i, 0)

    def own_copy(t):
        return pltpu.make_async_copy(summed[t], piece(t, 0, 0), ag_l.at[t])

    def second_copies(t):
        return [
            remote(
                summed[t], piece(t, 0, 0),
                ag_s.at[t, 1], ag_r.at[t, 1, i - 1], along(i, False),
            )
            for i in (2, 1, 3)
        ]

    def first_copies(t, i):
        return [
            remote(
                held(t, i), piece(t, i, 0),
                ag_s.at[t, 2], first_r.at[t, i, j - 1], along(j, True),
            )
            for j in (2, 1, 3)
        ]

    def core_copy(t, i, j):
        return remote(
            held(t, i) if j == 0 else piece(t, i, j), piece(t, i, j),
            ag_s.at[t, 3], other_r.at[t], (g, zh * 2 + 1 - c),
        )

    def gather_start(t):
        for k in range(3):
            wait_for(met[t].at[0], ag_r.at[t, 0, k])
        for chunk in range(2):
            for to_zh in range(2):
                summed[t][chunk * 2 + to_zh] = (
                    met[t][to_zh, chunk] + met[t][2 + to_zh, chunk]
                ).astype(BF)
        for copy in second_copies(t) + first_copies(t, 0):
            copy.start()
        core_copy(t, 0, 0).start()
        own_copy(t).start()

    def gather_pass(t):
        for i in (1, 3, 2):
            wait_for(piece(t, i, 0), ag_r.at[t, 1, i - 1])
            for copy in first_copies(t, i):
                copy.start()
            core_copy(t, i, 0).start()

    def gather_core(t):
        for i in (0, 1, 3, 2):
            for j in (1, 3, 2):
                wait_for(piece(t, i, j), first_r.at[t, i, j - 1])
                core_copy(t, i, j).start()

    def gather_end(t):
        own_copy(t).wait()
        wait_for(gathered[t].at[1 - c], other_r.at[t])

    def attend_back(u, qi, ki, masked):
        lane = lax.broadcasted_iota(jnp.int32, (256, 128), 1)
        for half in range(2):
            keys = pl.ds(half * 256, 256)
            first_q = 256 if masked and half == 1 else 0
            d_v, d_k = [], []
            for head in range(2):
                d_w = mm(vn[ki, keys, :], dom[qi, head, :, first_q:])
                d_s = (d_w * fc[u, head, keys, first_q:].astype(F32)).astype(BF)
                d_v.append(mm(wc[u, head, keys, first_q:], don[qi, first_q:, :]))
                d_k.append(mm(d_s, qn[qi, first_q:, :]))
                part = mm(act[ki, 384 + head * 64 : 448 + head * 64, keys], d_s)
                lanes = slice(head * 64, head * 64 + 64)
                if half == 0:
                    out_u[u, lanes, :] = part
                else:
                    out_u[u, lanes, first_q:] += part
            dv_u[u, keys, :] = jnp.where(lane < 64, d_v[0], d_v[1])
            dk_u[u, keys, :] = jnp.where(lane < 64, d_k[0], d_k[1])

    def finish(q):
        d_q, d_k, d_v = out_u[q], dk_u[q], dv_u[q]
        if q == 0:
            d_k = d_k + in_a * (dk_u[4] + dk_u[5])
            d_v = d_v + in_a * (dv_u[4] + dv_u[5])
        if q == 1:
            d_q = d_q + in_a * out_u[4]
            d_k = d_k + dk_u[6] + in_b * dk_u[5]
            d_v = d_v + dv_u[6] + in_b * dv_u[5]
        if q == 2:
            d_q = d_q + out_u[6] + in_a * out_u[5]
            d_k = d_k + in_b * dk_u[4]
            d_v = d_v + in_b * dv_u[4]
        if q == 3:
            d_q = d_q + in_b * (out_u[4] + out_u[5])
        dpre[q, 128:256, :] = (2.0 * d_v.T * slope[q, 128:256, :]).astype(BF)
        dpre[q, 256:384, :] = (0.125 * d_q * slope[q, 256:384, :]).astype(BF)
        dpre[q, 384:512, :] = (d_k.T * slope[q, 384:512, :]).astype(BF)

    def dx_core(k):
        return remote(
            dxs.at[k], dxp.at[k], dxc_s.at[0], dxc_r.at[k], (g, zh * 2 + 1 - c)
        )

    def to_partner(k):
        q = 3 * (1 - c) if k == 0 else 1 + c
        dxs[k] = mm(dpre[q], wt[...], TN).astype(BF)
        dx_core(k).start()

    def rows_of(zl_, h):
        return pl.ds(pl.multiple_of(zl_ * 256 + h * 128, 128), 128)

    def dx_across(k, h):
        to_zh = c if k == 0 else 1 - c
        code = jnp.where(to_zh == zh, 0, 1)
        return remote(
            dxs.at[2 + k, rows_of(1 - zl, h)], zr.at[code, h],
            dxz_s.at[0], dxz_r.at[code, h],
            (grp(x, 1 - zl, y), to_zh * 2 + c),
        )

    def dx_same(k, h):
        return remote(
            dxs.at[2 + k, rows_of(zl, h)], zr.at[2, h], dxz_s.at[0], dxz_r.at[2, h],
            (g, (1 - zh) * 2 + c),
        )

    def to_planes(k):
        q = 3 * c if k == 0 else 2 - c
        to_zh = c if k == 0 else 1 - c
        mine = mm(dpre[q], wt[...], TN)
        wait_for(dxp.at[k], dxc_r.at[k])
        both = (mine + dxp[k].astype(F32)).astype(BF)
        back = jnp.where(
            lax.broadcasted_iota(jnp.int32, (512, 512), 0) == slot_of(places[q]), 1.0, 0.0
        ).astype(BF)
        dxs[2 + k] = mm(back, both).astype(BF)

        for h in range(2):

            @pl.when(to_zh != zh)
            def _(h=h):
                dx_same(k, h).start()

            dx_across(k, h).start()

    @pl.loop(0, 2)
    def _(f):
        attend_back(4 + f, query_of(f), key_of(f), False)

    @pl.loop(0, 2)
    def _(i):
        attend_back(3 * i, 3 * i, 3 * i, True)

    finish(0)
    finish(3)
    to_partner(0)
    meet(0)
    for q in (0, 3):
        part = mm(dpre[q, 128:, :], x_all[q])
        if q == 0:
            acc[...] = part
        else:
            acc[...] += part
    to_planes(0)

    @pl.loop(1, 3)
    def _(q):
        attend_back(q, q, q, True)

    gather_start(0)
    attend_back(6, 2, 1, False)
    finish(1)
    finish(2)
    to_partner(1)
    total = acc[...] + mm(dpre[1, 128:, :], x_all[1]) + mm(dpre[2, 128:, :], x_all[2])
    for b in range(3):
        gl_s[:, :, :, b] = (
            total[b * 128 : (b + 1) * 128].T.astype(BF).reshape(4, 2, 4, 16, 128)
        )
    grads_out(gl_s, gl_r, gl_sem)
    to_planes(1)

    def go_home(h):
        for k in range(3):
            wait_for(zr.at[k, h], dxz_r.at[k, h])
        keep = jnp.where(c == zh, 2, 3)
        own = (dxs[keep, rows_of(zl, h)].astype(F32) + zr[2, h].astype(F32)).astype(BF)
        other = (zr[0, h].astype(F32) + zr[1, h].astype(F32)).astype(BF)
        fin[pl.ds(zl, 1), slots(h)] = own.reshape(1, 8, 16, 512)
        fin[pl.ds(1 - zl, 1), slots(h)] = other.reshape(1, 8, 16, 512)

        @pl.loop(1 - h, 8)
        def _(j):
            i = j + 8 * h
            tx, ty = shifted(i, -1)
            remote(
                fin.at[:, i], dx_out.at[x, :, y], home_sem.at[0], home_sem.at[1],
                (grp(tx, zl, ty), s),
            ).start()

        if h == 0:
            pltpu.make_async_copy(fin.at[:, 0], dx_out.at[x, :, y], home_sem.at[1]).start()

    for a in range(2):
        wait_for(rows.at[a, c, 0:2, 0, 0:15], plane_s.at[a])
        wait_for(rows.at[a, c, :, 0], z_s.at[a])
        wait_for(rows.at[a, c, 0:2], core_s.at[a])
    wait_for(places.at[0:3], seq_s.at[0])
    wait_for(stats.at[0:3], seq_s.at[1])
    wait_for(dxs.at[0:2], dxc_s.at[0])
    wait_for(ge_r.at[0:15], ge_sem.at[0])
    meet(1)
    wait_for(gl_r.at[0:15], gl_sem.at[0])
    gather_pass(0)
    gather_start(1)
    gather_pass(1)
    go_home(0)
    go_home(1)
    gather_core(0)
    gather_core(1)
    gather_end(0)
    gather_end(1)

    wait_for(dx_out, home_sem.at[1])
    wait_for(fin.at[:, 0:15], home_sem.at[0])
    wait_for(zr, dxz_s.at[0])
    for t in range(2):
        wait_for(met[t].at[0:3], ag_s.at[t, 0])
        wait_for(gathered[t].at[0, 0, 0:3], ag_s.at[t, 1])
        wait_for(gathered[t].at[0, 0:3], ag_s.at[t, 2])
        wait_for(gathered[t].at[0], ag_s.at[t, 3])


def finish_kernel(dx_ref, dy_ref, e_ref, l_ref, dx_out, gin_out, gout_out, e, l, dxv, dyv, gin, gout, sem, out_sem):
    factor = 1.0 / 256.0
    loads = []
    for core, axis in ((1, 0), (1, 1), (1, 2), (1, 3), (0, 0), (0, 1), (0, 2), (0, 3)):
        k = len(loads)
        loads.append(
            (
                pltpu.make_async_copy(e_ref.at[core, axis], e.at[core, axis], sem.at[0, k]),
                pltpu.make_async_copy(l_ref.at[core, axis], l.at[core, axis], sem.at[1, k]),
            )
        )
        for copy in loads[-1]:
            copy.start()
    rows_in = (
        pltpu.make_async_copy(dx_ref, dxv, sem.at[0, 8]),
        pltpu.make_async_copy(dy_ref, dyv, sem.at[1, 8]),
    )
    for copy in rows_in:
        copy.start()
    for pair in loads[:4]:
        for copy in pair:
            copy.wait()
    stores = []
    for x in range(4):
        for copy in loads[4 + x]:
            copy.wait()
        for core in range(2):
            for y in range(4):
                for z in range(4):
                    position = (z % 2) * 2 + core
                    at = (core, x, y, z) if core == 0 else (core, y, x, z)
                    row = x * 128 + (z // 2) * 64 + y * 16
                    for b in range(4):
                        tile = e[*at, 0] if b == 0 else l[*at, b - 1]
                        lo = b * 512 + position * 128
                        gin[row : row + 16, lo : lo + 128] = tile.astype(F32) * factor
                    row = position * 128 + (z // 2) * 64 + y * 16
                    gout[row : row + 16, x * 128 : x * 128 + 128] = (
                        e[*at, 1].astype(F32) * factor
                    )
        part = slice(x * 128, x * 128 + 128)
        stores.append(
            pltpu.make_async_copy(gin.at[part], gin_out.at[part], out_sem.at[x])
        )
        stores[-1].start()
    for x in range(2):
        part = slice(x * 256, x * 256 + 256)
        stores.append(
            pltpu.make_async_copy(gout.at[part], gout_out.at[part], out_sem.at[4 + x])
        )
        stores[-1].start()
    for copy in rows_in:
        copy.wait()
    dxv[...] = (dxv[...].astype(F32) + dyv[...].astype(F32)).astype(BF)
    stores.append(pltpu.make_async_copy(dxv, dx_out, out_sem.at[6]))
    stores[-1].start()
    for copy in stores:
        copy.wait()


def per_device(x_home, dy_home, w_in, w_out, place, seg_ids):
    shape = (4, 2, 4, 16, 512)
    vm = pltpu.VMEM
    dma = pltpu.SemaphoreType.DMA
    hbm = pl.BlockSpec(memory_space=pl.ANY)
    in_vmem = pl.BlockSpec(memory_space=pltpu.VMEM)
    dx, early, late = pl.pallas_call(
        kernel,
        out_shape=(
            jax.ShapeDtypeStruct(shape, BF),
            jax.ShapeDtypeStruct((2, 4, 4, 4, 2, 16, 128), BF),
            jax.ShapeDtypeStruct((2, 4, 4, 4, 3, 16, 128), BF),
        ),
        in_specs=[
            hbm, hbm, hbm, hbm, in_vmem, pl.BlockSpec(memory_space=pltpu.SMEM),
        ],
        out_specs=(hbm, hbm, hbm),
        scratch_shapes=[
            vm((2, 2, 3, 2, 16, 16, 512), BF),
            vm((4, 512, 512), BF),
            vm((4, 512, 512), BF),
            vm((4, 512, 512), BF),
            vm((4, 512, 512), BF),
            vm((4, 512, 512), F32),
            vm((4, 2, 128, 512), BF),
            vm((4, 512, 128), BF),
            vm((4, 512, 128), BF),
            vm((4, 512, 128), BF),
            vm((7, 2, 512, 512), BF),
            vm((7, 2, 512, 512), BF),
            vm((7, 128, 512), F32),
            vm((4, 128, 512), F32),
            vm((4, 128, 512), F32),
            vm((4, 4, 4, 512), F32),
            vm((4, 2, 128, 512), BF),
            vm((4, 512, 128), BF),
            vm((7, 512, 128), F32),
            vm((7, 512, 128), F32),
            vm((4, 512, 512), BF),
            vm((512, 512), BF),
            vm((512, 512), BF),
            vm((128, 512), BF),
            vm((4, 1, 512), jnp.int32),
            vm((4, 2, 4, 2, 16, 128), BF),
            vm((16, 2, 2, 16, 128), BF),
            vm((4, 2, 4, 3, 16, 128), BF),
            vm((16, 2, 3, 16, 128), BF),
            vm((4, 2, 2, 16, 128), F32),
            vm((4, 2, 16, 128), BF),
            vm((4, 2, 3, 16, 128), F32),
            vm((4, 3, 16, 128), BF),
            vm((384, 512), F32),
            vm((4, 512, 512), BF),
            vm((2, 512, 512), BF),
            vm((3, 2, 128, 512), BF),
            vm((2, 16, 16, 512), BF),
            dma((6,)), dma((2,)), dma((2, 2)), dma((2,)), dma((2, 3, 2)),
            dma((2,)), dma((2, 4, 2)), dma((2,)), dma((2, 3)), dma((2,)), dma((2,)),
            dma((2, 4)), dma((2, 2, 3)), dma((2,)), dma((2, 4, 3)), dma((2,)),
            dma((1,)), dma((2,)), dma((1,)), dma((3, 2)), dma((2,)),
        ],
        compiler_params=pltpu.CompilerParams(
            collective_id=0, has_side_effects=True, vmem_limit_bytes=63 * 2**20
        ),
    )(
        x_home.reshape(shape),
        dy_home.reshape(shape),
        w_in,
        w_out,
        place.reshape(1, 512),
        seg_ids.reshape(1, 2048),
    )
    return pl.pallas_call(
        finish_kernel,
        out_shape=(
            jax.ShapeDtypeStruct((512, 512), BF),
            jax.ShapeDtypeStruct((512, 2048), F32),
            jax.ShapeDtypeStruct((512, 512), F32),
        ),
        in_specs=[hbm, hbm, hbm, hbm],
        out_specs=(hbm, hbm, hbm),
        scratch_shapes=[
            vm((2, 4, 4, 4, 2, 16, 128), BF),
            vm((2, 4, 4, 4, 3, 16, 128), BF),
            vm((512, 512), BF),
            vm((512, 512), BF),
            vm((512, 2048), F32),
            vm((512, 512), F32),
            dma((2, 9)),
            dma((7,)),
        ],
        compiler_params=pltpu.CompilerParams(vmem_limit_bytes=62 * 2**20),
    )(dx.reshape(512, 512), dy_home, early, late)


def solution(mesh):
    in_specs = (
        P(("grp", "seq"), None),
        P(("grp", "seq"), None),
        P(),
        P(),
        P("grp", "seq", None),
        P("grp", None),
    )
    out_specs = (P(("grp", "seq"), None), P(), P())
    return jax.shard_map(
        per_device, mesh=mesh, in_specs=in_specs, out_specs=out_specs, check_vma=False
    )
```

```python
import jax
import jax.numpy as jnp
from jax import lax
from jax.experimental import pallas as pl
from jax.experimental.pallas import tpu as pltpu
from jax.sharding import PartitionSpec as P

BF = jnp.bfloat16
F32 = jnp.float32
MESH = pl.DeviceIdType.MESH
NN = (((1,), (0,)), ((), ()))
NT = (((1,), (1,)), ((), ()))
TN = (((0,), (0,)), ((), ()))


def mm(a, b, dims=NN):
    return lax.dot_general(a, b, dims, preferred_element_type=F32)


def remote(src, dst, send, recv, device):
    return pltpu.make_async_remote_copy(
        src_ref=src,
        dst_ref=dst,
        send_sem=send,
        recv_sem=recv,
        device_id=device,
        device_id_type=MESH,
    )


def wait_for(ref, sem):
    pltpu.make_async_copy(ref, ref, sem).wait()


def kernel(
    x_ref, dy_ref, win_ref, wout_ref, place_ref, seg_ref,
    dx_out, age, agl,
    rows, perm, x_all, dy_all, act, slope, qm, qn, kn, vn, wc, fc, out_u, out_t, dm_t, stats,
    dom, don, dv_u, dk_u, dpre, wsl, wt, wo, places,
    ge_s, ge_r, gl_s, gl_r, met_e, mine_e, met_l, mine_l, acc, dxs, dxp, zr, fin,
    local_sem, plane_s, plane_r, z_s, z_r, core_s, core_r, seq_s, seq_r, ge_sem, gl_sem,
    ag_s, ag_r, ag_l, first_r, other_r, dxc_s, dxc_r, dxz_s, dxz_r, home_sem,
):
    g = lax.axis_index("grp")
    s = lax.axis_index("seq")
    x, zl, y = g // 8, (g // 4) % 2, g % 4
    zh, c = s // 2, s % 2

    def grp(x_, zl_, y_):
        return (x_ * 2 + zl_) * 4 + y_

    weight_copies = []
    for b in range(4):
        weight_copies.append(
            pltpu.make_async_copy(
                win_ref.at[:, pl.ds(pl.multiple_of(b * 512 + s * 128, 128), 128)],
                wsl.at[:, b * 128 : (b + 1) * 128],
                local_sem.at[b],
            )
        )
    weight_copies.append(
        pltpu.make_async_copy(
            wout_ref.at[pl.ds(pl.multiple_of(s * 128, 128), 128)], wo, local_sem.at[4]
        )
    )
    for copy in weight_copies:
        copy.start()

    barrier = pltpu.get_barrier_semaphore()

    def shifted(i, sign):
        return lax.rem(x + 4 + sign * (i // 4), 4), lax.rem(y + 4 + sign * lax.rem(i, 4), 4)

    @pl.loop(1, 16)
    def _(i):
        tx, ty = shifted(i, 1)
        pl.semaphore_signal(
            barrier, inc=1, device_id=(grp(tx, zl, ty), s), device_id_type=MESH
        )

    for i in range(1, 4):
        pl.semaphore_signal(
            barrier, inc=1, device_id=(g, lax.rem(s + i, 4)), device_id_type=MESH
        )
    for to_zh in range(2):
        pl.semaphore_signal(
            barrier, inc=1, device_id=(grp(x, 1 - zl, y), to_zh * 2 + c), device_id_type=MESH
        )
    pl.semaphore_wait(barrier, 20)

    homes = (x_ref, dy_ref)
    for a in range(2):
        for h in range(2):

            @pl.loop(1 - h, 8)
            def _(j, a=a, h=h):
                i = j + 8 * h
                tx, ty = shifted(i, 1)
                remote(
                    homes[a].at[tx, :, ty],
                    rows.at[a, c, pl.ds(zl, 2), zh, i],
                    plane_s.at[a],
                    plane_r.at[a, h],
                    (grp(tx, zl, ty), s),
                ).start()

            if h == 0:
                pltpu.make_async_copy(
                    homes[a].at[x, :, y], rows.at[a, c, pl.ds(zl, 2), zh, 0], plane_r.at[a, 0]
                ).start()
        if a == 0:
            pltpu.make_async_copy(place_ref, places.at[s], local_sem.at[5]).start()
            for i in range(1, 4):
                remote(
                    place_ref,
                    places.at[s],
                    seq_s.at[0],
                    seq_r.at[0, i - 1],
                    (g, lax.rem(s + i, 4)),
                ).start()

    z_peers = (
        (grp(x, 1 - zl, y), s),
        (grp(x, 1 - zl, y), (1 - zh) * 2 + c),
        (g, (1 - zh) * 2 + c),
    )

    def slots(h):
        return slice(8 * h, 8 * h + 8)

    def block(a, core, zl_, zh_, h):
        return rows.at[a, core, 2 * zl_, zh_, slots(h)]

    def z_out(a, k, h):
        src = rows.at[a, c, 1, zh, slots(h)] if k < 2 else block(a, c, zl, zh, h)
        return remote(
            src, block(a, c, zl, zh, h), z_s.at[a], z_r.at[a, k, h], z_peers[k]
        )

    where_from = ((1 - zl, zh), (1 - zl, 1 - zh), (zl, 1 - zh), (zl, zh))

    def core_out(a, k, h):
        ref = block(a, c, *where_from[k], h)
        return remote(
            ref, ref, core_s.at[a], core_r.at[a, k, h], (g, zh * 2 + 1 - c)
        )

    def spread_plane(a, h):
        wait_for(rows.at[a, c, pl.ds(zl, 2), zh, slots(h)], plane_r.at[a, h])
        for k in range(3):
            z_out(a, k, h).start()
        core_out(a, 3, h).start()

    def forward(a, k, h):
        wait_for(block(a, c, *where_from[k], h), z_r.at[a, k, h])
        core_out(a, k, h).start()

    def from_core(a, k):
        for h in range(2):
            wait_for(block(a, 1 - c, *where_from[k], h), core_r.at[a, k, h])

    for copy in weight_copies:
        copy.wait()
    wt[...] = wsl[...].T
    spread_plane(0, 0)
    spread_plane(0, 1)

    wait_for(places.at[0], local_sem.at[5])
    for i in range(1, 4):
        wait_for(places.at[0], seq_r.at[0, i - 1])

    def slot_of(p):
        apart = ((x - (p >> 7)) & 3) * 4 + ((y - (p >> 4)) & 3)
        return ((p >> 6) & 1) * 256 + apart * 16 + (p & 15)

    @pl.loop(0, 4)
    def _(q):
        slot = slot_of(places[q])
        column = jnp.broadcast_to(slot.astype(F32), (128, 512)).T
        lane = lax.broadcasted_iota(jnp.int32, (512, 128), 1).astype(F32)
        for b in range(4):
            perm[q, :, b * 128 : (b + 1) * 128] = jnp.where(
                column == lane + float(b * 128), 1.0, 0.0
            ).astype(BF)

    def ordered(a, q):
        low = rows[a, lax.rem(q, 2), 0, q // 2].reshape(256, 512)
        high = rows[a, lax.rem(q, 2), 2, q // 2].reshape(256, 512)
        return (mm(perm[q, :, :256], low) + mm(perm[q, :, 256:], high)).astype(BF)

    def project(q):
        x_all[q] = ordered(0, q)
        for b in range(4):
            pre = mm(wt[b * 128 : (b + 1) * 128, :], x_all[q], NT)
            sig = 0.5 * jnp.tanh(0.5 * pre) + 0.5
            full = pre * sig
            slope[q, b * 128 : (b + 1) * 128, :] = sig + full * (1.0 - sig)
            cut = full.astype(BF)
            act[q, b * 128 : (b + 1) * 128, :] = cut
            if b == 1:
                vn[q] = cut.T
            if b == 2:
                qn[q] = (cut * BF(0.125)).T
                scaled = cut * BF(0.0625)
                zero = jnp.zeros((64, 512), BF)
                qm[q, 0] = jnp.concatenate([scaled[:64], zero], axis=0)
                qm[q, 1] = jnp.concatenate([zero, scaled[64:]], axis=0)
            if b == 3:
                kn[q] = cut.T

    is_a = seg_ref[0, 0] == seg_ref[0, 1535]
    in_a = jnp.where(is_a, 1.0, 0.0).astype(F32)
    in_b = 1.0 - in_a
    long, short = 1.0 / 1536.0, 1.0 / 512.0
    inv_len = (
        in_a * long + in_b * short, long, long, in_a * short + in_b * long
    )

    def query_of(f):
        return jnp.where(f == 2, 2, jnp.where(is_a, f + 1, 3))

    def key_of(f):
        return jnp.where(f == 2, 1, jnp.where(is_a, 0, 2 - f))

    def causal(rows_, cols):
        return lax.broadcasted_iota(jnp.int32, (rows_, cols), 0) <= lax.broadcasted_iota(
            jnp.int32, (rows_, cols), 1
        )

    def weigh(u, qi, ki, head, half, first, masked):
        keys = pl.ds(half * 256, 256)
        h = mm(kn[ki, keys, :], qm[qi, head, :, first:])
        t = jnp.tanh(h)
        a = 1.0 + t
        w = h * a
        f = a * (1.0 - w) + (w + w)
        if masked:
            keep = causal(256, 512 - first)
            w = jnp.where(keep, w, 0.0)
            f = jnp.where(keep, f, 0.0)
        w = w.astype(BF)
        wc[u, head, keys, first:] = w
        fc[u, head, keys, first:] = f.astype(BF)
        return mm(act[ki, 128 + head * 64 : 192 + head * 64, keys], w)

    def diagonal(q):
        for head in range(2):
            lanes = slice(head * 64, head * 64 + 64)
            out_u[q, lanes, :] = weigh(q, q, q, head, 0, 0, True)
            out_u[q, lanes, 256:] += weigh(q, q, q, head, 1, 256, True)

    forward(0, 0, 0)
    forward(0, 0, 1)
    spread_plane(1, 0)
    forward(0, 1, 0)
    forward(0, 2, 0)
    spread_plane(1, 1)
    from_core(0, 3)
    from_core(0, 0)

    @pl.loop(0, 2)
    def _(j):
        project(zh * 2 + j)

    forward(0, 1, 1)
    forward(0, 2, 1)

    @pl.loop(0, 2)
    def _(j):
        diagonal(zh * 2 + j)

    from_core(0, 1)
    from_core(0, 2)

    @pl.loop(0, 2)
    def _(j):
        project((1 - zh) * 2 + j)

    forward(1, 0, 0)
    forward(1, 0, 1)

    @pl.loop(0, 2)
    def _(j):
        diagonal((1 - zh) * 2 + j)

    def across(f):
        qi, ki = query_of(f), key_of(f)
        for head in range(2):
            lanes = slice(head * 64, head * 64 + 64)
            out_u[4 + f, lanes, :] = weigh(4 + f, qi, ki, head, 0, 0, False) + weigh(
                4 + f, qi, ki, head, 1, 0, False
            )

    @pl.loop(0, 2)
    def _(f):
        across(f)

    for k in (1, 2):
        forward(1, k, 0)
    across(2)

    def sums(q):
        dy_all[q] = ordered(1, q)
        d_mixed = mm(wo[...], dy_all[q], NT)
        dm_t[q] = d_mixed
        with_4 = jnp.where(q == 1, in_a, jnp.where(q == 3, in_b, 0.0))
        with_5 = jnp.where(q == 2, in_a, jnp.where(q == 3, in_b, 0.0))
        with_6 = jnp.where(q == 2, 1.0, 0.0)
        total = out_u[q] + with_4 * out_u[4] + with_5 * out_u[5] + with_6 * out_u[6]
        total = total * jnp.where(q == 0, inv_len[0], jnp.where(q == 3, inv_len[3], long))
        out_t[q] = total
        centre = jnp.mean(total, axis=0, keepdims=True)
        away = total - centre
        d_normed = d_mixed * act[q, :128, :].astype(F32)
        stats[s, q, 0:1, :] = centre
        stats[s, q, 1:2, :] = jnp.sum(away * away, axis=0, keepdims=True)
        stats[s, q, 2:3, :] = jnp.sum(d_normed, axis=0, keepdims=True)
        stats[s, q, 3:4, :] = jnp.sum(d_normed * away, axis=0, keepdims=True)

    from_core(1, 3)
    from_core(1, 0)

    @pl.loop(0, 2)
    def _(j):
        sums(zh * 2 + j)

    for k in (1, 2):
        forward(1, k, 1)
    from_core(1, 1)
    from_core(1, 2)

    @pl.loop(0, 2)
    def _(j):
        sums((1 - zh) * 2 + j)

    def stats_out(i):
        return remote(
            stats.at[s], stats.at[s], seq_s.at[1], seq_r.at[1, i - 1],
            (g, lax.rem(s + i, 4)),
        )

    for i in range(1, 4):
        stats_out(i).start()
    for i in range(1, 4):
        wait_for(stats.at[lax.rem(s + i, 4)], seq_r.at[1, 3 - i])

    centres = [stats[r, :, 0, :] for r in range(4)]
    mean_all = (centres[0] + centres[1] + centres[2] + centres[3]) * 0.25
    square = jnp.zeros_like(mean_all)
    plain = jnp.zeros_like(mean_all)
    cross = jnp.zeros_like(mean_all)
    for r in range(4):
        off = centres[r] - mean_all
        square += stats[r, :, 1, :] + 128.0 * off * off
        plain += stats[r, :, 2, :]
        cross += stats[r, :, 3, :] + off * stats[r, :, 2, :]
    spread_all = lax.rsqrt(square * (1.0 / 512.0) + 1e-5)
    plain = plain * (1.0 / 512.0)
    cross = cross * spread_all * (1.0 / 512.0)

    grad_out = jnp.zeros((128, 512), F32)
    grad_u = jnp.zeros((128, 512), F32)
    for q in range(4):
        gate = act[q, :128, :].astype(F32)
        spread = spread_all[q : q + 1]
        normed = (out_t[q] - mean_all[q : q + 1]) * spread
        d_mixed = dm_t[q]
        mixed = (normed * gate).astype(BF)
        d_u = (d_mixed * normed * slope[q, :128, :]).astype(BF)
        dpre[q, :128, :] = d_u
        d_out = (
            (d_mixed * gate - plain[q : q + 1] - normed * cross[q : q + 1])
            * (spread * (0.5 * inv_len[q]))
        ).astype(BF)
        zero = jnp.zeros((64, 512), BF)
        dom[q, 0] = jnp.concatenate([d_out[:64], zero], axis=0)
        dom[q, 1] = jnp.concatenate([zero, d_out[64:]], axis=0)
        don[q] = d_out.T
        grad_out += mm(mixed, dy_all[q])
        grad_u += mm(d_u, x_all[q])

    def grads_out(buf, got, sem):
        for low, high in ((8, 16), (1, 8)):

            @pl.loop(low, high)
            def _(i):
                tx, ty = shifted(i, 1)
                remote(
                    buf.at[tx, :, ty], got.at[i], sem.at[0], sem.at[1],
                    (grp(tx, zl, ty), s),
                ).start()

        pltpu.make_async_copy(buf.at[x, :, y], got.at[0], sem.at[1]).start()

    ge_s[:, :, :, 0] = grad_u.T.astype(BF).reshape(4, 2, 4, 16, 128)
    for b in range(4):
        ge_s[b, :, :, 1] = (
            grad_out[:, b * 128 : (b + 1) * 128].astype(BF).reshape(2, 4, 16, 128)
        )
    grads_out(ge_s, ge_r, ge_sem)

    first = jnp.where(c == 0, x, y)
    second = jnp.where(c == 0, y, x)
    zz = zl * 2 + zh
    reduced = ((ge_r, ge_sem), (gl_r, gl_sem))
    met = (met_e, met_l)
    summed = (mine_e, mine_l)
    gathered = (age, agl)

    def z_copies(t):
        ref = met[t].at[zz]
        return [
            remote(ref, ref, ag_s.at[t, 0], ag_r.at[t, 0, k], peer)
            for k, peer in enumerate(z_peers)
        ]

    def meet(t):
        got, sem = reduced[t]
        wait_for(got, sem.at[1])
        met[t][zz] = jnp.sum(got[...].astype(F32), axis=0).astype(BF)
        for copy in z_copies(t):
            copy.start()

    def along(i, on_first):
        nf = lax.rem(first + i, 4) if on_first else first
        ns = second if on_first else lax.rem(second + i, 4)
        nx = jnp.where(c == 0, nf, ns)
        ny = jnp.where(c == 0, ns, nf)
        return (grp(nx, zl, ny), s)

    def piece(t, i, j):
        return gathered[t].at[
            c, lax.rem(first + 4 - j, 4), lax.rem(second + 4 - i, 4)
        ]

    def held(t, i):
        return summed[t] if i == 0 else piece(t, i, 0)

    def own_copy(t):
        return pltpu.make_async_copy(summed[t], piece(t, 0, 0), ag_l.at[t])

    def second_copies(t):
        return [
            remote(
                summed[t], piece(t, 0, 0),
                ag_s.at[t, 1], ag_r.at[t, 1, i - 1], along(i, False),
            )
            for i in (2, 1, 3)
        ]

    def first_copies(t, i):
        return [
            remote(
                held(t, i), piece(t, i, 0),
                ag_s.at[t, 2], first_r.at[t, i, j - 1], along(j, True),
            )
            for j in (2, 1, 3)
        ]

    def core_copy(t, i, j):
        return remote(
            held(t, i) if j == 0 else piece(t, i, j), piece(t, i, j),
            ag_s.at[t, 3], other_r.at[t], (g, zh * 2 + 1 - c),
        )

    def gather_start(t):
        for k in range(3):
            wait_for(met[t].at[0], ag_r.at[t, 0, k])
        for chunk in range(2):
            for to_zh in range(2):
                summed[t][chunk * 2 + to_zh] = (
                    met[t][to_zh, chunk].astype(F32) + met[t][2 + to_zh, chunk].astype(F32)
                ).astype(BF)
        for copy in second_copies(t) + first_copies(t, 0):
            copy.start()
        core_copy(t, 0, 0).start()
        own_copy(t).start()

    def gather_pass(t):
        for i in (1, 3, 2):
            wait_for(piece(t, i, 0), ag_r.at[t, 1, i - 1])
            for copy in first_copies(t, i):
                copy.start()
            core_copy(t, i, 0).start()

    def gather_core(t):
        for i in (0, 1, 3, 2):
            for j in (1, 3, 2):
                wait_for(piece(t, i, j), first_r.at[t, i, j - 1])
                core_copy(t, i, j).start()

    def gather_end(t):
        own_copy(t).wait()
        wait_for(gathered[t].at[1 - c], other_r.at[t])

    def attend_back(u, qi, ki, masked):
        lane = lax.broadcasted_iota(jnp.int32, (256, 128), 1)
        for half in range(2):
            keys = pl.ds(half * 256, 256)
            first_q = 256 if masked and half == 1 else 0
            d_v, d_k = [], []
            for head in range(2):
                d_w = mm(vn[ki, keys, :], dom[qi, head, :, first_q:])
                d_s = (d_w * fc[u, head, keys, first_q:].astype(F32)).astype(BF)
                d_v.append(mm(wc[u, head, keys, first_q:], don[qi, first_q:, :]))
                d_k.append(mm(d_s, qn[qi, first_q:, :]))
                part = mm(act[ki, 384 + head * 64 : 448 + head * 64, keys], d_s)
                lanes = slice(head * 64, head * 64 + 64)
                if half == 0:
                    out_u[u, lanes, :] = part
                else:
                    out_u[u, lanes, first_q:] += part
            dv_u[u, keys, :] = jnp.where(lane < 64, d_v[0], d_v[1])
            dk_u[u, keys, :] = jnp.where(lane < 64, d_k[0], d_k[1])

    def finish(q):
        d_q, d_k, d_v = out_u[q], dk_u[q], dv_u[q]
        if q == 0:
            d_k = d_k + in_a * (dk_u[4] + dk_u[5])
            d_v = d_v + in_a * (dv_u[4] + dv_u[5])
        if q == 1:
            d_q = d_q + in_a * out_u[4]
            d_k = d_k + dk_u[6] + in_b * dk_u[5]
            d_v = d_v + dv_u[6] + in_b * dv_u[5]
        if q == 2:
            d_q = d_q + out_u[6] + in_a * out_u[5]
            d_k = d_k + in_b * dk_u[4]
            d_v = d_v + in_b * dv_u[4]
        if q == 3:
            d_q = d_q + in_b * (out_u[4] + out_u[5])
        dpre[q, 128:256, :] = (2.0 * d_v.T * slope[q, 128:256, :]).astype(BF)
        dpre[q, 256:384, :] = (0.125 * d_q * slope[q, 256:384, :]).astype(BF)
        dpre[q, 384:512, :] = (d_k.T * slope[q, 384:512, :]).astype(BF)

    def dx_core(k):
        return remote(
            dxs.at[k], dxp.at[k], dxc_s.at[0], dxc_r.at[k], (g, zh * 2 + 1 - c)
        )

    def to_partner(k):
        q = 3 * (1 - c) if k == 0 else 1 + c
        dxs[k] = mm(dpre[q], wt[...], TN).astype(BF)
        dx_core(k).start()

    def rows_of(zl_, h):
        return pl.ds(pl.multiple_of(zl_ * 256 + h * 128, 128), 128)

    def dx_across(k, h):
        to_zh = c if k == 0 else 1 - c
        code = jnp.where(to_zh == zh, 0, 1)
        return remote(
            dxs.at[2 + k, rows_of(1 - zl, h)], zr.at[code, h],
            dxz_s.at[0], dxz_r.at[code, h],
            (grp(x, 1 - zl, y), to_zh * 2 + c),
        )

    def dx_same(k, h):
        return remote(
            dxs.at[2 + k, rows_of(zl, h)], zr.at[2, h], dxz_s.at[0], dxz_r.at[2, h],
            (g, (1 - zh) * 2 + c),
        )

    def to_planes(k):
        q = 3 * c if k == 0 else 2 - c
        to_zh = c if k == 0 else 1 - c
        mine = mm(dpre[q], wt[...], TN)
        wait_for(dxp.at[k], dxc_r.at[k])
        both = (mine + dxp[k].astype(F32)).astype(BF)
        back = jnp.where(
            lax.broadcasted_iota(jnp.int32, (512, 512), 0) == slot_of(places[q]), 1.0, 0.0
        ).astype(BF)
        dxs[2 + k] = mm(back, both).astype(BF)

        for h in range(2):

            @pl.when(to_zh != zh)
            def _(h=h):
                dx_same(k, h).start()

            dx_across(k, h).start()

    @pl.loop(0, 2)
    def _(f):
        attend_back(4 + f, query_of(f), key_of(f), False)

    @pl.loop(0, 2)
    def _(i):
        attend_back(3 * i, 3 * i, 3 * i, True)

    finish(0)
    finish(3)
    to_partner(0)
    meet(0)
    for q in (0, 3):
        part = mm(dpre[q, 128:, :], x_all[q])
        if q == 0:
            acc[...] = part
        else:
            acc[...] += part
    to_planes(0)

    @pl.loop(1, 3)
    def _(q):
        attend_back(q, q, q, True)

    gather_start(0)
    attend_back(6, 2, 1, False)
    finish(1)
    finish(2)
    to_partner(1)
    total = acc[...] + mm(dpre[1, 128:, :], x_all[1]) + mm(dpre[2, 128:, :], x_all[2])
    for b in range(3):
        gl_s[:, :, :, b] = (
            total[b * 128 : (b + 1) * 128].T.astype(BF).reshape(4, 2, 4, 16, 128)
        )
    grads_out(gl_s, gl_r, gl_sem)
    to_planes(1)

    def go_home(h):
        for k in range(3):
            wait_for(zr.at[k, h], dxz_r.at[k, h])
        keep = jnp.where(c == zh, 2, 3)
        own = (dxs[keep, rows_of(zl, h)].astype(F32) + zr[2, h].astype(F32)).astype(BF)
        other = (zr[0, h].astype(F32) + zr[1, h].astype(F32)).astype(BF)
        fin[pl.ds(zl, 1), slots(h)] = own.reshape(1, 8, 16, 512)
        fin[pl.ds(1 - zl, 1), slots(h)] = other.reshape(1, 8, 16, 512)

        @pl.loop(1 - h, 8)
        def _(j):
            i = j + 8 * h
            tx, ty = shifted(i, -1)
            remote(
                fin.at[:, i], dx_out.at[x, :, y], home_sem.at[0], home_sem.at[1],
                (grp(tx, zl, ty), s),
            ).start()

        if h == 0:
            pltpu.make_async_copy(fin.at[:, 0], dx_out.at[x, :, y], home_sem.at[1]).start()

    for a in range(2):
        wait_for(rows.at[a, c, 0:2, 0, 0:15], plane_s.at[a])
        wait_for(rows.at[a, c, :, 0], z_s.at[a])
        wait_for(rows.at[a, c, 0:2], core_s.at[a])
    wait_for(places.at[0:3], seq_s.at[0])
    wait_for(stats.at[0:3], seq_s.at[1])
    wait_for(dxs.at[0:2], dxc_s.at[0])
    wait_for(ge_r.at[0:15], ge_sem.at[0])
    meet(1)
    wait_for(gl_r.at[0:15], gl_sem.at[0])
    gather_pass(0)
    gather_start(1)
    gather_pass(1)
    go_home(0)
    go_home(1)
    gather_core(0)
    gather_core(1)
    gather_end(0)
    gather_end(1)

    wait_for(dx_out, home_sem.at[1])
    wait_for(fin.at[:, 0:15], home_sem.at[0])
    wait_for(zr, dxz_s.at[0])
    for t in range(2):
        wait_for(met[t].at[0:3], ag_s.at[t, 0])
        wait_for(gathered[t].at[0, 0, 0:3], ag_s.at[t, 1])
        wait_for(gathered[t].at[0, 0:3], ag_s.at[t, 2])
        wait_for(gathered[t].at[0], ag_s.at[t, 3])


def finish_kernel(dx_ref, dy_ref, e_ref, l_ref, dx_out, gin_out, gout_out, e, l, dxv, dyv, gin, gout, sem, out_sem):
    factor = 1.0 / 256.0
    loads = []
    for core, axis in ((1, 0), (1, 1), (1, 2), (1, 3), (0, 0), (0, 1), (0, 2), (0, 3)):
        k = len(loads)
        loads.append(
            (
                pltpu.make_async_copy(e_ref.at[core, axis], e.at[core, axis], sem.at[0, k]),
                pltpu.make_async_copy(l_ref.at[core, axis], l.at[core, axis], sem.at[1, k]),
            )
        )
        for copy in loads[-1]:
            copy.start()
    rows_in = (
        pltpu.make_async_copy(dx_ref, dxv, sem.at[0, 8]),
        pltpu.make_async_copy(dy_ref, dyv, sem.at[1, 8]),
    )
    for copy in rows_in:
        copy.start()
    for pair in loads[:4]:
        for copy in pair:
            copy.wait()
    stores = []
    for x in range(4):
        for copy in loads[4 + x]:
            copy.wait()
        for core in range(2):
            for y in range(4):
                for z in range(4):
                    position = (z % 2) * 2 + core
                    at = (core, x, y, z) if core == 0 else (core, y, x, z)
                    row = x * 128 + (z // 2) * 64 + y * 16
                    for b in range(4):
                        tile = e[*at, 0] if b == 0 else l[*at, b - 1]
                        lo = b * 512 + position * 128
                        gin[row : row + 16, lo : lo + 128] = tile.astype(F32) * factor
                    row = position * 128 + (z // 2) * 64 + y * 16
                    gout[row : row + 16, x * 128 : x * 128 + 128] = (
                        e[*at, 1].astype(F32) * factor
                    )
        part = slice(x * 128, x * 128 + 128)
        stores.append(
            pltpu.make_async_copy(gin.at[part], gin_out.at[part], out_sem.at[x])
        )
        stores[-1].start()
    for x in range(2):
        part = slice(x * 256, x * 256 + 256)
        stores.append(
            pltpu.make_async_copy(gout.at[part], gout_out.at[part], out_sem.at[4 + x])
        )
        stores[-1].start()
    for copy in rows_in:
        copy.wait()
    dxv[...] = (dxv[...].astype(F32) + dyv[...].astype(F32)).astype(BF)
    stores.append(pltpu.make_async_copy(dxv, dx_out, out_sem.at[6]))
    stores[-1].start()
    for copy in stores:
        copy.wait()


def per_device(x_home, dy_home, w_in, w_out, place, seg_ids):
    shape = (4, 2, 4, 16, 512)
    vm = pltpu.VMEM
    dma = pltpu.SemaphoreType.DMA
    hbm = pl.BlockSpec(memory_space=pl.ANY)
    in_vmem = pl.BlockSpec(memory_space=pltpu.VMEM)
    dx, early, late = pl.pallas_call(
        kernel,
        out_shape=(
            jax.ShapeDtypeStruct(shape, BF),
            jax.ShapeDtypeStruct((2, 4, 4, 4, 2, 16, 128), BF),
            jax.ShapeDtypeStruct((2, 4, 4, 4, 3, 16, 128), BF),
        ),
        in_specs=[
            hbm, hbm, hbm, hbm, in_vmem, pl.BlockSpec(memory_space=pltpu.SMEM),
        ],
        out_specs=(hbm, hbm, hbm),
        scratch_shapes=[
            vm((2, 2, 3, 2, 16, 16, 512), BF),
            vm((4, 512, 512), BF),
            vm((4, 512, 512), BF),
            vm((4, 512, 512), BF),
            vm((4, 512, 512), BF),
            vm((4, 512, 512), F32),
            vm((4, 2, 128, 512), BF),
            vm((4, 512, 128), BF),
            vm((4, 512, 128), BF),
            vm((4, 512, 128), BF),
            vm((7, 2, 512, 512), BF),
            vm((7, 2, 512, 512), BF),
            vm((7, 128, 512), F32),
            vm((4, 128, 512), F32),
            vm((4, 128, 512), F32),
            vm((4, 4, 4, 512), F32),
            vm((4, 2, 128, 512), BF),
            vm((4, 512, 128), BF),
            vm((7, 512, 128), F32),
            vm((7, 512, 128), F32),
            vm((4, 512, 512), BF),
            vm((512, 512), BF),
            vm((512, 512), BF),
            vm((128, 512), BF),
            vm((4, 1, 512), jnp.int32),
            vm((4, 2, 4, 2, 16, 128), BF),
            vm((16, 2, 2, 16, 128), BF),
            vm((4, 2, 4, 3, 16, 128), BF),
            vm((16, 2, 3, 16, 128), BF),
            vm((4, 2, 2, 16, 128), BF),
            vm((4, 2, 16, 128), BF),
            vm((4, 2, 3, 16, 128), BF),
            vm((4, 3, 16, 128), BF),
            vm((384, 512), F32),
            vm((4, 512, 512), BF),
            vm((2, 512, 512), BF),
            vm((3, 2, 128, 512), BF),
            vm((2, 16, 16, 512), BF),
            dma((6,)), dma((2,)), dma((2, 2)), dma((2,)), dma((2, 3, 2)),
            dma((2,)), dma((2, 4, 2)), dma((2,)), dma((2, 3)), dma((2,)), dma((2,)),
            dma((2, 4)), dma((2, 2, 3)), dma((2,)), dma((2, 4, 3)), dma((2,)),
            dma((1,)), dma((2,)), dma((1,)), dma((3, 2)), dma((2,)),
        ],
        compiler_params=pltpu.CompilerParams(
            collective_id=0, has_side_effects=True, vmem_limit_bytes=63 * 2**20
        ),
    )(
        x_home.reshape(shape),
        dy_home.reshape(shape),
        w_in,
        w_out,
        place.reshape(1, 512),
        seg_ids.reshape(1, 2048),
    )
    return pl.pallas_call(
        finish_kernel,
        out_shape=(
            jax.ShapeDtypeStruct((512, 512), BF),
            jax.ShapeDtypeStruct((512, 2048), F32),
            jax.ShapeDtypeStruct((512, 512), F32),
        ),
        in_specs=[hbm, hbm, hbm, hbm],
        out_specs=(hbm, hbm, hbm),
        scratch_shapes=[
            vm((2, 4, 4, 4, 2, 16, 128), BF),
            vm((2, 4, 4, 4, 3, 16, 128), BF),
            vm((512, 512), BF),
            vm((512, 512), BF),
            vm((512, 2048), F32),
            vm((512, 512), F32),
            dma((2, 9)),
            dma((7,)),
        ],
        compiler_params=pltpu.CompilerParams(vmem_limit_bytes=62 * 2**20),
    )(dx.reshape(512, 512), dy_home, early, late)


def solution(mesh):
    in_specs = (
        P(("grp", "seq"), None),
        P(("grp", "seq"), None),
        P(),
        P(),
        P("grp", "seq", None),
        P("grp", None),
    )
    out_specs = (P(("grp", "seq"), None), P(), P())
    return jax.shard_map(
        per_device, mesh=mesh, in_specs=in_specs, out_specs=out_specs, check_vma=False
    )
```
